256 devices in a mesh: ctx: 8 (over z_lo, core), exp: 32 (over z_hi, x, y).
Axes of the slice: x: 4, y: 4, z: 8 (z_hi: 2, z_lo: 4; z = z_hi * 4 + z_lo), core: 2. Of those that a mesh axis runs over, the one named last changes fastest.
Arguments:
- queries: bfloat16 [1024, 12288], P('ctx', 'exp'), may hold values from -160 to 160
- latents: bfloat16 [1024, 512], P('ctx'), may hold values from -6 to 6
- rotary_keys: bfloat16 [1024, 64], P('ctx'), may hold values from -5 to 5
- block_order: int32 [8], replicated, may hold values from 0 to 7, each once
- absorb_key: bfloat16 [64, 128, 512], P('exp'), may hold values from -0.5 to 0.5
- absorb_value: bfloat16 [64, 512, 128], P('exp'), may hold values from -0.25 to 0.25
- output_weight: bfloat16 [8192, 7168], P('exp', 'ctx'), may hold values from -0.0625 to 0.0625
- residual: bfloat16 [1024, 7168], P(('ctx', 'exp')), may hold values from -6 to 6
- norm_gain: bfloat16 [7168], replicated, may hold values from 0.25 to 1.75
- route_experts: int32 [1024, 8], replicated, may hold values from 0 to 31, all different within a row; in each aligned block of 128 rows (0 to 127, 128 to 255, ...) at most 40 rows name the same one
- route_weights: float32 [1024, 8], replicated, may hold values from 0.1 to 0.6
- gate_weight: bfloat16 [7168, 65536], P(None, ('ctx', 'exp')), may hold values from -0.0625 to 0.0625
- up_weight: bfloat16 [7168, 65536], P(None, ('ctx', 'exp')), may hold values from -0.0625 to 0.0625
- down_weight: bfloat16 [65536, 7168], P(('ctx', 'exp')), may hold values from -0.125 to 0.125
Outputs:
- block_output: float32 [1024, 7168], P(('ctx', 'exp'))
The draws below stay inside these ranges and needn't reach their ends.
Inputs may be any that keep to these rules, and one draw needn't show every extreme that they name: `route_experts`: within each context block (aligned blocks of 128 rows) no expert is named by more than 40 rows, a bound that some block reaches. `block_order`: each block number appears once.
All inputs are finite; a program needn't handle non-finite values.
Results may differ from the reference program's by a relative error of at most 0.019.
Values may be sent and summed in bfloat16 or wider, within the bound.
No kernel may reach another device: no remote copies, remote signals or barrier semaphores. Data moves between devices by JAX's collectives and lax.ppermute only.
A program may use at most 128 MiB of HBM per device.

```python
import math
import jax
import jax.numpy as jnp
import numpy as np
from jax import lax

D = 7168
HEADS = 64
NOPE = 128
ROPE = 64
LAT = 512
VDIM = 128
FF = 2048
EXPERTS = 32
TOPK = 8
BLOCK = 128
BLOCKS = 8
TOKENS = 1024
FF_DEV = 256
CAPACITY = 40


def rotary_table(key):
    gauss = jnp.clip(jax.random.normal(jax.random.fold_in(key, 101), (TOKENS, ROPE), jnp.float32), -5.0, 5.0)
    table = gauss
    return table


def draw_queries(key, part):
    key = jax.random.fold_in(key, 7)
    values = 0.6 * jnp.clip(jax.random.normal(key, (TOKENS, HEADS, NOPE + ROPE), jnp.float32), -5.0, 5.0)
    return values.reshape(TOKENS, HEADS * (NOPE + ROPE)).astype(jnp.bfloat16)


def draw_rotary_keys(key, part):
    table = rotary_table(key)
    return table.astype(jnp.bfloat16)


def draw_residual(key, part):
    key = jax.random.fold_in(key, 11)
    row_scale = jnp.exp(jax.random.uniform(jax.random.fold_in(key, 1), (TOKENS, 1), jnp.float32, -1.15, 1.15))
    column_scale = jnp.exp(jax.random.uniform(jax.random.fold_in(key, 2), (1, D), jnp.float32, -1.15, 1.15))
    values = 0.05 * row_scale * column_scale * jnp.clip(jax.random.normal(jax.random.fold_in(key, 4), (TOKENS, D), jnp.float32), -5.0, 5.0)
    return values.astype(jnp.bfloat16)


def block_levels(rng, shape, pieces, low, top_value):
    gain = 1.0
    for axis_at, shards_of in pieces:
        heights = jax.random.uniform(jax.random.fold_in(jax.random.fold_in(rng, 6), axis_at), (shards_of,), jnp.float32, low / len(pieces), top_value / len(pieces))
        gain = gain * jnp.repeat(jnp.exp(heights), shape[axis_at] // shards_of).reshape((-1,) + (1,) * (len(shape) - 1 - axis_at))
    return gain


def assign_block(key, own, number, rows, amount, top, reach, slope):
    ranking = jax.random.permutation(key, amount)
    heavy_load, usual = load_shares(amount, rows * top, reach, slope, True), load_shares(amount, rows * top, reach, slope, False)
    places = jnp.arange(amount)

    def named(lengths, offset_by):
        used = int((lengths > 0).sum())
        fixed = max(1, used // 4)
        passed = fixed + (places - fixed + offset_by * (used - fixed)) % max(1, amount - fixed)
        return jnp.zeros((amount,), jnp.int32).at[ranking[jnp.where(places < fixed, places, passed)]].set(jnp.asarray(lengths, jnp.int32))

    lengths = jnp.where(number % 4 == 0, named(heavy_load, number // 4), named(usual, number - number // 4 - 1))
    mixed = jax.random.permutation(jax.random.fold_in(own, 3), amount)
    giver, receiver = mixed[0:amount // 2 * 2:2], mixed[1:amount // 2 * 2:2]
    slack = jnp.minimum(lengths[giver] - 1, reach - lengths[receiver]) // 2
    slack = jnp.where((giver == ranking[0]) | (receiver == ranking[0]) | (lengths[receiver] == 0), 0, jnp.maximum(slack, 0))
    passed = jax.random.randint(jax.random.fold_in(own, 4), (amount // 2,), 0, 1 << 20) % (slack + 1)
    lengths = lengths.at[giver].add(-passed).at[receiver].add(passed)
    items = jnp.searchsorted(jnp.cumsum(lengths), jnp.arange(rows * top), side="right").astype(jnp.int32)
    listing = items.reshape(top, rows).T
    listing = listing[jax.random.permutation(jax.random.fold_in(own, 1), rows)]
    offset_by = jax.random.randint(jax.random.fold_in(own, 2), (rows, 1), 0, top)
    return jnp.take_along_axis(listing, (jnp.arange(top)[None, :] + offset_by) % top, axis=1)


def load_shares(amount, total, most, skew, full):
    weights = [(1 << 20) // math.isqrt(standing ** skew) + 1 for standing in range(1, amount + 1)]
    largest = most if full else min(most, max(-(-total // amount), total * weights[0] // sum(weights)))
    least = 1 if total - largest >= amount - 1 else 0
    counts, rest = [largest] + [least] * (amount - 1), total - largest - least * (amount - 1)
    while rest > 0:
        free = [i for i in range(1, amount) if counts[i] < largest] or [i for i in range(1, amount) if counts[i] < most]
        pool, left = sum([weights[i] for i in free]), rest
        for i in free:
            more = min(most - counts[i], max(1, left * weights[i] // pool), rest)
            counts[i] = counts[i] + more
            rest = rest - more
    return np.array(counts)


def normal_values(key, shape, deviation, reach, shards=(), kind=jnp.bfloat16):
    gain = block_levels(key, shape, shards, -0.22, 0.18) if shards else 1.0
    drawn = jax.random.normal(key, shape, jnp.float32) * deviation * gain
    return jnp.minimum(jnp.maximum(drawn, -reach), reach).astype(kind)


def setup_inputs(seed: int = 0) -> dict:
    arg_keys = jax.random.split(jax.random.key(seed), 15)
    queries = draw_queries(jax.random.fold_in(arg_keys[14], 71), 0)
    latents = normal_values(arg_keys[1], (TOKENS, LAT), 1.0, 6.0, ((0, 8),))
    rotary_keys = draw_rotary_keys(jax.random.fold_in(arg_keys[14], 71), 0)
    block_order = jax.random.permutation(arg_keys[3], BLOCKS).astype(jnp.int32)
    absorb_key = normal_values(arg_keys[4], (HEADS, NOPE, LAT), NOPE ** -0.5, 0.5, ((0, 32),))
    absorb_value = normal_values(arg_keys[5], (HEADS, LAT, VDIM), LAT ** -0.5, 0.25, ((0, 32),))
    output_weight = normal_values(arg_keys[6], (HEADS * VDIM, D), (HEADS * VDIM) ** -0.5, 0.0625, ((0, 32), (1, 8)))
    residual = draw_residual(jax.random.fold_in(arg_keys[14], 71), 0)
    norm_gain = jnp.clip(1.0 + 0.15 * jax.random.normal(arg_keys[8], (D,), jnp.float32), 0.25, 1.75).astype(jnp.bfloat16)
    route_experts_keys = jax.random.split(jax.random.fold_in(arg_keys[9], 1), TOKENS // BLOCK)
    route_experts_turns = jax.random.permutation(jax.random.fold_in(arg_keys[9], 3), TOKENS // BLOCK)
    route_experts = jax.vmap(lambda own, number: assign_block(jax.random.fold_in(arg_keys[9], 2), own, number, BLOCK, EXPERTS, TOPK, CAPACITY, 2))(route_experts_keys, route_experts_turns).reshape((TOKENS, TOPK))
    route_weights = jnp.clip(jax.random.uniform(arg_keys[10], (TOKENS, TOPK), jnp.float32, 0.1, 0.6), 0.1, 0.6)
    gate_weight = normal_values(arg_keys[11], (D, EXPERTS * FF), D ** -0.5, 0.0625, ((1, 256),))
    up_weight = normal_values(arg_keys[12], (D, EXPERTS * FF), D ** -0.5, 0.0625, ((1, 256),))
    down_weight = normal_values(arg_keys[13], (EXPERTS * FF, D), FF ** -0.5, 0.125, ((0, 256),))
    return dict(queries=queries, latents=latents, rotary_keys=rotary_keys, block_order=block_order, absorb_key=absorb_key, absorb_value=absorb_value, output_weight=output_weight, residual=residual, norm_gain=norm_gain, route_experts=route_experts, route_weights=route_weights, gate_weight=gate_weight, up_weight=up_weight, down_weight=down_weight)


EPSILON = 1e-06

def token_positions(block_order):
    row_index = jnp.arange(TOKENS, dtype=jnp.int32)
    return block_order[row_index // BLOCK].astype(jnp.int32) * BLOCK + row_index % BLOCK

def reference(queries, latents, rotary_keys, block_order, absorb_key, absorb_value, output_weight, residual, norm_gain, route_experts, route_weights, gate_weight, up_weight, down_weight):
    score_scale = 1.0 / math.sqrt(NOPE + ROPE)
    shaped = queries.reshape(TOKENS, HEADS, NOPE + ROPE)
    position = token_positions(block_order)
    visible = position[None, :] <= position[:, None]

    def head_output(head_index):
        query_plain = shaped[:, head_index, :NOPE]
        query_rotary = shaped[:, head_index, NOPE:]
        query_latent = jnp.dot(query_plain, absorb_key[head_index], preferred_element_type=jnp.float32).astype(jnp.bfloat16)
        scores = jnp.dot(query_latent, latents.T, preferred_element_type=jnp.float32)
        scores = scores + jnp.dot(query_rotary, rotary_keys.T, preferred_element_type=jnp.float32)
        scores = jnp.where(visible, scores * score_scale, -1e+30)
        row_max = lax.optimization_barrier(jnp.max(scores, axis=1, keepdims=True))
        exponent = jnp.where(visible, jnp.exp(scores - row_max), 0.0)
        row_sum = lax.optimization_barrier(jnp.sum(exponent, axis=1, keepdims=True))
        mixture = jnp.dot(exponent.astype(jnp.bfloat16), latents, preferred_element_type=jnp.float32)
        out_latent = (mixture / row_sum).astype(jnp.bfloat16)
        return jnp.dot(out_latent, absorb_value[head_index], preferred_element_type=jnp.float32).astype(jnp.bfloat16)
    head_values = lax.map(head_output, jnp.arange(HEADS, dtype=jnp.int32))
    flattened = jnp.transpose(head_values, (1, 0, 2)).reshape(TOKENS, HEADS * VDIM)
    residual_sum = residual.astype(jnp.float32) + jnp.dot(flattened, output_weight, preferred_element_type=jnp.float32)
    normed = (residual_sum * lax.rsqrt(lax.optimization_barrier(jnp.mean(residual_sum * residual_sum, axis=1, keepdims=True)) + EPSILON) * norm_gain.astype(jnp.float32)).astype(jnp.bfloat16)
    matches = route_experts[:, :, None] == jnp.arange(EXPERTS, dtype=jnp.int32)[None, None, :]
    combine = lax.optimization_barrier(jnp.sum(jnp.where(matches, route_weights[:, :, None], jnp.float32(0.0)), axis=1))
    group_count = FF // FF_DEV

    def one_expert(running_total, expert_index):
        first_col = (expert_index * FF).astype(jnp.int32)
        gate_pre = jnp.dot(normed, lax.dynamic_slice_in_dim(gate_weight, first_col, FF, 1), preferred_element_type=jnp.float32)
        up_pre = jnp.dot(normed, lax.dynamic_slice_in_dim(up_weight, first_col, FF, 1), preferred_element_type=jnp.float32)
        activated = (jax.nn.silu(gate_pre) * up_pre).astype(jnp.bfloat16)
        down_rows = lax.dynamic_slice_in_dim(down_weight, first_col, FF, 0)

        def one_group(group_total, group_index):
            start_unit = (group_index * FF_DEV).astype(jnp.int32)
            piece_cols = lax.dynamic_slice_in_dim(activated, start_unit, FF_DEV, 1)
            piece_rows = lax.dynamic_slice_in_dim(down_rows, start_unit, FF_DEV, 0)
            rounded = lax.optimization_barrier(jnp.dot(piece_cols, piece_rows, preferred_element_type=jnp.float32).astype(jnp.bfloat16))
            return (group_total + rounded.astype(jnp.float32), None)
        summed, _ = lax.scan(one_group, jnp.zeros((TOKENS, D), jnp.float32), jnp.arange(group_count, dtype=jnp.int32))
        weight_column = lax.dynamic_slice_in_dim(combine, expert_index.astype(jnp.int32), 1, 1)
        return (running_total + weight_column * summed, None)
    expert_total, _ = lax.scan(one_expert, jnp.zeros((TOKENS, D), jnp.float32), jnp.arange(EXPERTS, dtype=jnp.int32))
    return residual_sum + expert_total
```

```python
import math

import jax
import jax.numpy as jnp
from jax import lax
from jax.sharding import Mesh, PartitionSpec as P

FF = 2048
CAPACITY = 40
EPSILON = 1e-06

CTX = ("zl", "core")
EXP = ("zh", "x2", "x1", "y")
PATCH = ("x1", "y")
PLANE = ("x2", "x1", "y")
SIZES = (4, 2, 2, 2, 2, 4)


def all_to_all(value, axes):
    return lax.all_to_all(value, axes, split_axis=0, concat_axis=0, tiled=True)


def swap(value, axes, count, mask):
    return lax.ppermute(value, axes, [(i, i ^ mask) for i in range(count)])


def attend(queries, latents, rotary_keys, block_order, absorb_key, absorb_value):
    block_size = queries.shape[0]
    head_count, plain_width, latent_width = absorb_key.shape
    rotary_width = rotary_keys.shape[1]
    score_scale = 1.0 / math.sqrt(plain_width + rotary_width)
    keys = lax.all_gather(
        jnp.concatenate([latents, rotary_keys], axis=1), CTX, axis=0, tiled=True
    )
    ordered = jnp.arange(block_size, dtype=jnp.int32).reshape(2, 16, 4).transpose(1, 0, 2).reshape(-1)
    shaped = queries.reshape(2, 16, 4, head_count, plain_width + rotary_width)
    shaped = shaped.transpose(1, 0, 2, 3, 4).reshape(
        block_size, head_count, plain_width + rotary_width
    )
    here = lax.axis_index(CTX)
    order_here = jnp.sum(
        jnp.where(jnp.arange(block_order.shape[0], dtype=jnp.int32) == here, block_order, 0)
    )
    row_pos = jnp.tile(order_here * block_size + ordered, head_count)
    key_pos = (
        block_order[:, None] * block_size + jnp.arange(block_size, dtype=jnp.int32)[None, :]
    ).reshape(-1)
    query_latent = jnp.einsum(
        "thn,hnl->htl", shaped[:, :, :plain_width], absorb_key, preferred_element_type=jnp.float32
    ).astype(jnp.bfloat16)
    query = jnp.concatenate(
        [query_latent, shaped[:, :, plain_width:].transpose(1, 0, 2)], axis=2
    ).reshape(head_count * block_size, latent_width + rotary_width)
    scores = (
        jnp.einsum("rl,nl->rn", query, keys, preferred_element_type=jnp.float32) * score_scale
    )
    visible = key_pos[None, :] <= row_pos[:, None]
    scores = jnp.where(visible, scores, -1e30)
    row_max = jnp.max(scores, axis=1, keepdims=True)
    exponent = jnp.where(visible, jnp.exp(scores - row_max), 0.0)
    row_sum = jnp.sum(exponent, axis=1, keepdims=True)
    weighted = jnp.dot(
        exponent.astype(jnp.bfloat16),
        keys[:, :latent_width],
        preferred_element_type=jnp.float32,
    )
    out_latent = (
        (weighted / row_sum).astype(jnp.bfloat16).reshape(head_count, block_size, latent_width)
    )
    return (
        jnp.einsum("htl,hlv->thv", out_latent, absorb_value, preferred_element_type=jnp.float32)
        .astype(jnp.bfloat16)
        .reshape(block_size, -1)
    )


def on_device(
    queries,
    latents,
    rotary_keys,
    block_order,
    absorb_key,
    absorb_value,
    output_weight,
    residual,
    norm_gain,
    route_experts,
    route_weights,
    gate_weight,
    up_weight,
    down_weight,
):
    block_size = queries.shape[0]
    width = norm_gain.shape[0]
    share = output_weight.shape[1]
    hidden_share = gate_weight.shape[1]
    own_tokens = residual.shape[0]
    here = lax.axis_index(CTX)
    member = lax.axis_index(EXP)
    half = lax.axis_index("zh")
    patch_here = lax.axis_index(PATCH)

    down_parts = []
    for mask in range(8):
        piece = lax.dynamic_slice_in_dim(down_weight, (patch_here ^ mask) * share, share, 1)
        down_parts.append(swap(piece, PATCH, 8, mask) if mask else piece)

    head_values = attend(queries, latents, rotary_keys, block_order, absorb_key, absorb_value)
    gathered = lax.all_gather(head_values, CTX, axis=0)
    gathered = (
        gathered.reshape(8, 16, 8, -1).transpose(1, 0, 2, 3).reshape(8 * block_size, -1)
    )
    projected = jnp.dot(gathered, output_weight, preferred_element_type=jnp.float32).astype(
        jnp.bfloat16
    )
    landed = all_to_all(projected.reshape(16, 64, share), PLANE)
    partial = jnp.sum(landed.astype(jnp.float32), axis=0).reshape(8, 2, own_tokens, share)
    kept = lax.dynamic_index_in_dim(partial, half, 1, keepdims=False)
    given = lax.dynamic_index_in_dim(partial, 1 - half, 1, keepdims=False)
    summed = kept + swap(given.astype(jnp.bfloat16), "zh", 2, 1).astype(jnp.float32)
    rows = all_to_all(summed, CTX).transpose(1, 0, 2).reshape(own_tokens, width)
    residual_sum = rows + residual.astype(jnp.float32)
    normed = (
        residual_sum
        * lax.rsqrt(jnp.mean(residual_sum * residual_sum, axis=1, keepdims=True) + EPSILON)
        * norm_gain.astype(jnp.float32)
    ).astype(jnp.bfloat16)

    columns = normed.reshape(own_tokens, 8, share).transpose(1, 0, 2)
    spread = jnp.broadcast_to(columns[None], (4, 8, own_tokens, share)).reshape(
        32, own_tokens, share
    )
    block_columns = all_to_all(spread, EXP).reshape(block_size, share)

    owners = jnp.arange(8, dtype=jnp.int32) * 4 + member * hidden_share // FF
    own_experts = lax.dynamic_slice_in_dim(route_experts, here * block_size, block_size, 0)
    own_weights = lax.dynamic_slice_in_dim(route_weights, here * block_size, block_size, 0)
    matches = own_experts[None, :, :] == owners[:, None, None]
    chosen = jnp.any(matches, axis=2)
    gate_share = jnp.sum(jnp.where(matches, own_weights[None, :, :], 0.0), axis=2)
    before = jnp.dot(
        chosen.astype(jnp.bfloat16),
        jnp.triu(jnp.ones((block_size, block_size), jnp.bfloat16), 1),
        preferred_element_type=jnp.float32,
    ).astype(jnp.int32)
    selected = chosen[:, :, None] & (
        before[:, :, None] == jnp.arange(CAPACITY, dtype=jnp.int32)
    )
    outgoing = jnp.einsum(
        "rtc,td->rcd",
        selected.astype(jnp.bfloat16),
        block_columns,
        preferred_element_type=jnp.float32,
    ).astype(jnp.bfloat16)
    arrived = all_to_all(outgoing, CTX).reshape(8 * CAPACITY, share)

    gate_pre = jnp.zeros((8 * CAPACITY, hidden_share), jnp.float32)
    up_pre = jnp.zeros((8 * CAPACITY, hidden_share), jnp.float32)
    for mask in range(8):
        piece = swap(arrived, PATCH, 8, mask) if mask else arrived
        first = (patch_here ^ mask) * share
        gate_rows = lax.dynamic_slice_in_dim(gate_weight, first, share, 0)
        up_rows = lax.dynamic_slice_in_dim(up_weight, first, share, 0)
        gate_pre = gate_pre + jnp.dot(piece, gate_rows, preferred_element_type=jnp.float32)
        up_pre = up_pre + jnp.dot(piece, up_rows, preferred_element_type=jnp.float32)
    activated = (jax.nn.silu(gate_pre) * up_pre).astype(jnp.bfloat16)

    computed = jnp.zeros((8 * CAPACITY, share), jnp.float32)
    for mask in range(8):
        piece = swap(activated, PATCH, 8, mask) if mask else activated
        computed = computed + jnp.dot(piece, down_parts[mask], preferred_element_type=jnp.float32)
    returned = all_to_all(computed.astype(jnp.bfloat16).reshape(8, CAPACITY, share), CTX)
    weighing = jnp.where(selected, gate_share[:, :, None], 0.0).astype(jnp.bfloat16)
    block_total = jnp.dot(
        weighing.transpose(1, 0, 2).reshape(block_size, 8 * CAPACITY),
        returned.reshape(8 * CAPACITY, share),
        preferred_element_type=jnp.float32,
    ).astype(jnp.bfloat16)
    parts = all_to_all(block_total.reshape(32, own_tokens, share), EXP)
    expert_total = (
        jnp.sum(parts.reshape(4, 8, own_tokens, share).astype(jnp.float32), axis=0)
        .transpose(1, 0, 2)
        .reshape(own_tokens, width)
    )
    return residual_sum + expert_total


def solution(mesh):
    finer = Mesh(mesh.devices.reshape(SIZES), CTX + EXP)
    return jax.shard_map(
        on_device,
        mesh=finer,
        in_specs=(
            P(CTX, EXP),
            P(CTX, None),
            P(CTX, None),
            P(),
            P(EXP, None, None),
            P(EXP, None, None),
            P(EXP, CTX),
            P(CTX + EXP, None),
            P(),
            P(),
            P(),
            P(None, CTX + EXP),
            P(None, CTX + EXP),
            P(CTX + EXP, None),
        ),
        out_specs=P(CTX + EXP, None),
        check_vma=False,
    )
```

```python
import math

import jax
import jax.numpy as jnp
from jax import lax
from jax.sharding import Mesh, PartitionSpec as P

FF = 2048
CAPACITY = 40
EPSILON = 1e-06

CTX = ("zl", "core")
EXP = ("zh", "x2", "x1", "y")
PATCH = ("x1", "y")
PLANE = ("x2", "x1", "y")
SIZES = (4, 2, 2, 2, 2, 4)


def all_to_all(value, axes):
    return lax.all_to_all(value, axes, split_axis=0, concat_axis=0, tiled=True)


def swap(value, axes, count, mask):
    return lax.ppermute(value, axes, [(i, i ^ mask) for i in range(count)])


def gather_context(value):
    planes = [value] + [swap(value, "zl", 4, mask) for mask in range(1, 4)]
    mine = jnp.stack(planes)
    return jnp.concatenate([mine, swap(mine, "core", 2, 1)])


def sources(here):
    return here ^ jnp.array([0, 2, 4, 6, 1, 3, 5, 7], jnp.int32)


def by_context(value, here):
    shaped = value.reshape((2, 2, 2) + value.shape[1:])
    for axis, bit in ((0, 1), (1, 4), (2, 2)):
        shaped = jnp.where((here & bit) > 0, jnp.flip(shaped, axis), shaped)
    order = (1, 2, 0) + tuple(range(3, shaped.ndim))
    return shaped.transpose(order).reshape(value.shape)


def attend(queries, latents, rotary_keys, block_order, absorb_key, absorb_value):
    block_size = queries.shape[0]
    head_count, plain_width, latent_width = absorb_key.shape
    rotary_width = rotary_keys.shape[1]
    score_scale = 1.0 / math.sqrt(plain_width + rotary_width)
    keys = gather_context(jnp.concatenate([latents, rotary_keys], axis=1)).reshape(
        8 * block_size, latent_width + rotary_width
    )
    ordered = jnp.arange(block_size, dtype=jnp.int32).reshape(2, 16, 4).transpose(1, 0, 2).reshape(-1)
    shaped = queries.reshape(2, 16, 4, head_count, plain_width + rotary_width)
    shaped = shaped.transpose(1, 0, 2, 3, 4).reshape(
        block_size, head_count, plain_width + rotary_width
    )
    here = lax.axis_index(CTX)
    source_blocks = sources(here)
    source_order = jnp.sum(
        jnp.where(
            jnp.arange(8, dtype=jnp.int32)[None, :] == source_blocks[:, None],
            block_order[None, :],
            0,
        ),
        axis=1,
    )
    row_pos = jnp.tile(source_order[0] * block_size + ordered, head_count)
    key_pos = (
        source_order[:, None] * block_size + jnp.arange(block_size, dtype=jnp.int32)[None, :]
    ).reshape(-1)
    query_latent = jnp.einsum(
        "thn,hnl->htl", shaped[:, :, :plain_width], absorb_key, preferred_element_type=jnp.float32
    ).astype(jnp.bfloat16)
    query = jnp.concatenate(
        [query_latent, shaped[:, :, plain_width:].transpose(1, 0, 2)], axis=2
    ).reshape(head_count * block_size, latent_width + rotary_width)
    scores = (
        jnp.einsum("rl,nl->rn", query, keys, preferred_element_type=jnp.float32) * score_scale
    )
    visible = key_pos[None, :] <= row_pos[:, None]
    scores = jnp.where(visible, scores, -1e30)
    row_max = jnp.max(scores, axis=1, keepdims=True)
    exponent = jnp.where(visible, jnp.exp(scores - row_max), 0.0)
    row_sum = jnp.sum(exponent, axis=1, keepdims=True)
    weighted = jnp.dot(
        exponent.astype(jnp.bfloat16),
        keys[:, :latent_width],
        preferred_element_type=jnp.float32,
    )
    out_latent = (
        (weighted / row_sum).astype(jnp.bfloat16).reshape(head_count, block_size, latent_width)
    )
    return (
        jnp.einsum("htl,hlv->thv", out_latent, absorb_value, preferred_element_type=jnp.float32)
        .astype(jnp.bfloat16)
        .reshape(block_size, -1)
    )


def on_device(
    queries,
    latents,
    rotary_keys,
    block_order,
    absorb_key,
    absorb_value,
    output_weight,
    residual,
    norm_gain,
    route_experts,
    route_weights,
    gate_weight,
    up_weight,
    down_weight,
):
    block_size = queries.shape[0]
    width = norm_gain.shape[0]
    share = output_weight.shape[1]
    hidden_share = gate_weight.shape[1]
    own_tokens = residual.shape[0]
    here = lax.axis_index(CTX)
    member = lax.axis_index(EXP)
    half = lax.axis_index("zh")
    patch_here = lax.axis_index(PATCH)

    down_columns = all_to_all(
        down_weight.reshape(hidden_share, 8, share).transpose(1, 0, 2), PATCH
    )

    head_values = attend(queries, latents, rotary_keys, block_order, absorb_key, absorb_value)
    gathered = gather_context(head_values)
    gathered = (
        gathered.reshape(8, 16, 8, -1).transpose(1, 0, 2, 3).reshape(8 * block_size, -1)
    )
    projected = jnp.dot(gathered, output_weight, preferred_element_type=jnp.float32).astype(
        jnp.bfloat16
    )
    projected, down_columns = lax.optimization_barrier((projected, down_columns))
    landed = all_to_all(projected.reshape(16, 64, share), PLANE)
    partial = jnp.sum(landed.astype(jnp.float32), axis=0).reshape(8, 2, own_tokens, share)
    kept = lax.dynamic_index_in_dim(partial, half, 1, keepdims=False)
    given = lax.dynamic_index_in_dim(partial, 1 - half, 1, keepdims=False)
    summed = kept + swap(given.astype(jnp.bfloat16), "zh", 2, 1).astype(jnp.float32)
    rows = all_to_all(by_context(summed, here), CTX).transpose(1, 0, 2).reshape(own_tokens, width)
    residual_sum = rows + residual.astype(jnp.float32)
    normed = (
        residual_sum
        * lax.rsqrt(jnp.mean(residual_sum * residual_sum, axis=1, keepdims=True) + EPSILON)
        * norm_gain.astype(jnp.float32)
    ).astype(jnp.bfloat16)

    columns = normed.reshape(own_tokens, 8, share).transpose(1, 0, 2)
    spread = jnp.broadcast_to(columns[None], (4, 8, own_tokens, share)).reshape(
        32, own_tokens, share
    )
    block_columns = all_to_all(spread, EXP).reshape(block_size, share)

    owners = jnp.arange(8, dtype=jnp.int32) * 4 + member * hidden_share // FF
    own_experts = lax.dynamic_slice_in_dim(route_experts, here * block_size, block_size, 0)
    own_weights = lax.dynamic_slice_in_dim(route_weights, here * block_size, block_size, 0)
    matches = own_experts[None, :, :] == owners[:, None, None]
    chosen = jnp.any(matches, axis=2)
    gate_share = jnp.sum(jnp.where(matches, own_weights[None, :, :], 0.0), axis=2)
    before = jnp.dot(
        chosen.astype(jnp.bfloat16),
        jnp.triu(jnp.ones((block_size, block_size), jnp.bfloat16), 1),
        preferred_element_type=jnp.float32,
    ).astype(jnp.int32)
    selected = chosen[:, :, None] & (
        before[:, :, None] == jnp.arange(CAPACITY, dtype=jnp.int32)
    )
    outgoing = jnp.einsum(
        "rtc,td->rcd",
        selected.astype(jnp.bfloat16),
        block_columns,
        preferred_element_type=jnp.float32,
    ).astype(jnp.bfloat16)
    first_rows, last_rows = 24, CAPACITY - 24
    arrived_first = all_to_all(outgoing[:, :first_rows], CTX).reshape(8 * first_rows, share)
    arrived_last = all_to_all(outgoing[:, first_rows:], CTX).reshape(8 * last_rows, share)

    first_pieces = [arrived_first] + [swap(arrived_first, "y", 4, mask) for mask in range(1, 4)]
    pair = jnp.stack([arrived_last, swap(arrived_last, "x1", 2, 1)])
    pairs = [pair] + [swap(pair, "y", 4, mask) for mask in range(1, 4)]
    first_pieces = first_pieces + [swap(piece, "x1", 2, 1) for piece in first_pieces]
    last_pieces = [both[0] for both in pairs] + [both[1] for both in pairs]

    def activate(pieces):
        gate_pre, up_pre = 0.0, 0.0
        for mask, piece in enumerate(pieces):
            first = (patch_here ^ mask) * share
            gate_rows = lax.dynamic_slice_in_dim(gate_weight, first, share, 0)
            up_rows = lax.dynamic_slice_in_dim(up_weight, first, share, 0)
            gate_pre = gate_pre + jnp.dot(piece, gate_rows, preferred_element_type=jnp.float32)
            up_pre = up_pre + jnp.dot(piece, up_rows, preferred_element_type=jnp.float32)
        return (jax.nn.silu(gate_pre) * up_pre).astype(jnp.bfloat16)

    def share_and_return(activated, rows):
        spread = jnp.broadcast_to(activated[None], (8,) + activated.shape)
        hidden = all_to_all(spread, PATCH).transpose(1, 0, 2).reshape(8 * rows, 8 * hidden_share)
        computed = jnp.dot(
            hidden,
            down_columns.reshape(8 * hidden_share, share),
            preferred_element_type=jnp.float32,
        )
        return all_to_all(computed.astype(jnp.bfloat16).reshape(8, rows, share), CTX)

    returned = jnp.concatenate(
        [
            share_and_return(activate(first_pieces), first_rows),
            share_and_return(activate(last_pieces), last_rows),
        ],
        axis=1,
    )
    weighing = jnp.where(selected, gate_share[:, :, None], 0.0).astype(jnp.bfloat16)
    block_total = jnp.dot(
        weighing.transpose(1, 0, 2).reshape(block_size, 8 * CAPACITY),
        returned.reshape(8 * CAPACITY, share),
        preferred_element_type=jnp.float32,
    ).astype(jnp.bfloat16)
    parts = all_to_all(block_total.reshape(32, own_tokens, share), EXP)
    expert_total = (
        jnp.sum(parts.reshape(4, 8, own_tokens, share).astype(jnp.float32), axis=0)
        .transpose(1, 0, 2)
        .reshape(own_tokens, width)
    )
    return residual_sum + expert_total


def solution(mesh):
    finer = Mesh(mesh.devices.reshape(SIZES), CTX + EXP)
    return jax.shard_map(
        on_device,
        mesh=finer,
        in_specs=(
            P(CTX, EXP),
            P(CTX, None),
            P(CTX, None),
            P(),
            P(EXP, None, None),
            P(EXP, None, None),
            P(EXP, CTX),
            P(CTX + EXP, None),
            P(),
            P(),
            P(),
            P(None, CTX + EXP),
            P(None, CTX + EXP),
            P(CTX + EXP, None),
        ),
        out_specs=P(CTX + EXP, None),
        check_vma=False,
    )
```

```python
import math

import jax
import jax.numpy as jnp
from jax import lax
from jax.sharding import Mesh, PartitionSpec as P

FF = 2048
CAPACITY = 40
EPSILON = 1e-06

CTX = ("zl", "core")
EXP = ("zh", "x2", "x1", "y")
PATCH = ("x1", "y")
PLANE = ("x2", "x1", "y")
SIZES = (4, 2, 2, 2, 2, 4)


def all_to_all(value, axes):
    return lax.all_to_all(value, axes, split_axis=0, concat_axis=0, tiled=True)


def swap(value, axes, count, mask):
    return lax.ppermute(value, axes, [(i, i ^ mask) for i in range(count)])


def gather_context(value):
    planes = [value] + [swap(value, "zl", 4, mask) for mask in range(1, 4)]
    mine = jnp.stack(planes)
    return jnp.concatenate([mine, swap(mine, "core", 2, 1)])


def sources(here):
    return here ^ jnp.array([0, 2, 4, 6, 1, 3, 5, 7], jnp.int32)


def flip_groups(value, index):
    shaped = value.reshape((2, 2) + value.shape[1:])
    for axis, bit in ((0, 2), (1, 1)):
        shaped = jnp.where((index & bit) > 0, jnp.flip(shaped, axis), shaped)
    return shaped.reshape(value.shape)


def attend(queries, latents, rotary_keys, block_order, absorb_key, absorb_value):
    block_size = queries.shape[0]
    head_count, plain_width, latent_width = absorb_key.shape
    rotary_width = rotary_keys.shape[1]
    score_scale = 1.0 / math.sqrt(plain_width + rotary_width)
    keys = gather_context(jnp.concatenate([latents, rotary_keys], axis=1)).reshape(
        8 * block_size, latent_width + rotary_width
    )
    ordered = jnp.arange(block_size, dtype=jnp.int32).reshape(2, 16, 4).transpose(1, 0, 2).reshape(-1)
    shaped = queries.reshape(2, 16, 4, head_count, plain_width + rotary_width)
    shaped = shaped.transpose(1, 0, 2, 3, 4).reshape(
        block_size, head_count, plain_width + rotary_width
    )
    here = lax.axis_index(CTX)
    source_blocks = sources(here)
    source_order = jnp.sum(
        jnp.where(
            jnp.arange(8, dtype=jnp.int32)[None, :] == source_blocks[:, None],
            block_order[None, :],
            0,
        ),
        axis=1,
    )
    row_pos = jnp.tile(source_order[0] * block_size + ordered, head_count)
    key_pos = (
        source_order[:, None] * block_size + jnp.arange(block_size, dtype=jnp.int32)[None, :]
    ).reshape(-1)
    query_latent = jnp.einsum(
        "thn,hnl->htl", shaped[:, :, :plain_width], absorb_key, preferred_element_type=jnp.float32
    ).astype(jnp.bfloat16)
    query = jnp.concatenate(
        [query_latent, shaped[:, :, plain_width:].transpose(1, 0, 2)], axis=2
    ).reshape(head_count * block_size, latent_width + rotary_width)
    scores = (
        jnp.einsum("rl,nl->rn", query, keys, preferred_element_type=jnp.float32) * score_scale
    )
    visible = key_pos[None, :] <= row_pos[:, None]
    scores = jnp.where(visible, scores, -1e30)
    row_max = jnp.max(scores, axis=1, keepdims=True)
    exponent = jnp.where(visible, jnp.exp(scores - row_max), 0.0)
    row_sum = jnp.sum(exponent, axis=1, keepdims=True)
    weighted = jnp.dot(
        exponent.astype(jnp.bfloat16),
        keys[:, :latent_width],
        preferred_element_type=jnp.float32,
    )
    out_latent = (
        (weighted / row_sum).astype(jnp.bfloat16).reshape(head_count, block_size, latent_width)
    )
    return (
        jnp.einsum("htl,hlv->thv", out_latent, absorb_value, preferred_element_type=jnp.float32)
        .astype(jnp.bfloat16)
        .reshape(block_size, -1)
    )


def on_device(
    queries,
    latents,
    rotary_keys,
    block_order,
    absorb_key,
    absorb_value,
    output_weight,
    residual,
    norm_gain,
    route_experts,
    route_weights,
    gate_weight,
    up_weight,
    down_weight,
):
    block_size = queries.shape[0]
    width = norm_gain.shape[0]
    share = output_weight.shape[1]
    hidden_share = gate_weight.shape[1]
    own_tokens = residual.shape[0]
    here = lax.axis_index(CTX)
    member = lax.axis_index(EXP)
    patch_here = lax.axis_index(PATCH)

    early = hidden_share * 5 // 8
    down_early = all_to_all(
        down_weight[:early].reshape(early, 8, share).transpose(1, 0, 2), PATCH
    )

    owners = jnp.arange(8, dtype=jnp.int32) * 4 + member * hidden_share // FF
    own_experts = lax.dynamic_slice_in_dim(route_experts, here * block_size, block_size, 0)
    own_weights = lax.dynamic_slice_in_dim(route_weights, here * block_size, block_size, 0)
    matches = own_experts[None, :, :] == owners[:, None, None]
    chosen = jnp.any(matches, axis=2)
    gate_share = jnp.sum(jnp.where(matches, own_weights[None, :, :], 0.0), axis=2)
    before = jnp.dot(
        chosen.astype(jnp.bfloat16),
        jnp.triu(jnp.ones((block_size, block_size), jnp.bfloat16), 1),
        preferred_element_type=jnp.float32,
    ).astype(jnp.int32)
    selected = chosen[:, :, None] & (
        before[:, :, None] == jnp.arange(CAPACITY, dtype=jnp.int32)
    )
    group_here = lax.axis_index(("zh", "x2"))
    arranged = flip_groups(
        selected.astype(jnp.bfloat16).transpose(1, 0, 2).reshape(4, block_size // 4, 8, CAPACITY),
        group_here,
    ).reshape(block_size, 8, CAPACITY)
    weighing = jnp.where(selected, gate_share[:, :, None], 0.0).astype(jnp.bfloat16)
    weighing = weighing.transpose(1, 0, 2).reshape(block_size, 8 * CAPACITY)

    head_values = attend(queries, latents, rotary_keys, block_order, absorb_key, absorb_value)
    gathered = gather_context(head_values)
    gathered = (
        gathered.reshape(8, 16, 8, -1).transpose(1, 0, 2, 3).reshape(8 * block_size, -1)
    )
    projected = jnp.dot(gathered, output_weight, preferred_element_type=jnp.float32).astype(
        jnp.bfloat16
    )
    projected, down_early = lax.optimization_barrier((projected, down_early))
    landed = all_to_all(projected.reshape(16, 64, share), PLANE)
    late_rows = down_weight[early:].reshape(hidden_share - early, 8, share).transpose(1, 0, 2)
    landed, late_rows, arranged, weighing = lax.optimization_barrier(
        (landed, late_rows, arranged, weighing)
    )
    down_late = all_to_all(late_rows, PATCH)
    partial = jnp.sum(landed.astype(jnp.float32), axis=0).reshape(8, 2, own_tokens, share)
    half = lax.axis_index("zh")
    kept = lax.dynamic_index_in_dim(partial, half, 1, keepdims=False)
    given = lax.dynamic_index_in_dim(partial, 1 - half, 1, keepdims=False).astype(jnp.bfloat16)
    summed = kept + swap(given, "zh", 2, 1).astype(jnp.float32)
    columns_of = jnp.stack([summed[:4], swap(summed[4:], "core", 2, 1)], axis=1)
    columns_of = jnp.stack(
        [columns_of[0]] + [swap(columns_of[mask], "zl", 4, mask) for mask in range(1, 4)]
    ).reshape(2, 2, 2, own_tokens, share)
    for axis, bit in ((0, 4), (1, 2), (2, 1)):
        columns_of = jnp.where((here & bit) > 0, jnp.flip(columns_of, axis), columns_of)
    rows = columns_of.transpose(3, 0, 1, 2, 4).reshape(own_tokens, width)
    rows, down_late = lax.optimization_barrier((rows, down_late))
    residual_sum = rows + residual.astype(jnp.float32)
    normed = (
        residual_sum
        * lax.rsqrt(jnp.mean(residual_sum * residual_sum, axis=1, keepdims=True) + EPSILON)
        * norm_gain.astype(jnp.float32)
    ).astype(jnp.bfloat16)

    columns = normed.reshape(own_tokens, 8, share).transpose(1, 0, 2)
    group_columns = all_to_all(columns, PATCH).reshape(8 * own_tokens, share)
    block_columns = jnp.concatenate(
        [group_columns] + [swap(group_columns, ("zh", "x2"), 4, mask) for mask in range(1, 4)]
    )

    outgoing = jnp.einsum(
        "trc,td->rcd",
        arranged,
        block_columns,
        preferred_element_type=jnp.float32,
    ).astype(jnp.bfloat16)
    arrived = all_to_all(outgoing, CTX).reshape(8 * CAPACITY, share)

    split = 192
    beside = swap(arrived, "x1", 2, 1)
    first_pieces = [arrived[:split]] + [swap(arrived[:split], "y", 4, mask) for mask in range(1, 4)]
    first_pieces = (
        first_pieces
        + [beside[:split]]
        + [swap(piece, "x1", 2, 1) for piece in first_pieces[1:]]
    )
    pair = jnp.stack([arrived[split:], beside[split:]])
    pairs = [pair] + [swap(pair, "y", 4, mask) for mask in range(1, 4)]
    last_pieces = [both[0] for both in pairs] + [both[1] for both in pairs]

    weights = []
    for mask in range(8):
        first = (patch_here ^ mask) * share
        weights.append(
            jnp.concatenate(
                [
                    lax.dynamic_slice_in_dim(gate_weight, first, share, 0),
                    lax.dynamic_slice_in_dim(up_weight, first, share, 0),
                ],
                axis=1,
            )
        )

    def activate(pieces):
        pre = 0.0
        for piece, weight in zip(pieces, weights):
            pre = pre + jnp.dot(piece, weight, preferred_element_type=jnp.float32)
        return (jax.nn.silu(pre[:, :hidden_share]) * pre[:, hidden_share:]).astype(jnp.bfloat16)

    activated = jnp.concatenate([activate(first_pieces), activate(last_pieces)])
    hidden = all_to_all(
        jnp.broadcast_to(activated[None], (8,) + activated.shape), PATCH
    ).transpose(1, 0, 2)
    computed = jnp.dot(
        hidden[:, :, :early].reshape(8 * CAPACITY, 8 * early),
        down_early.reshape(8 * early, share),
        preferred_element_type=jnp.float32,
    ) + jnp.dot(
        hidden[:, :, early:].reshape(8 * CAPACITY, 8 * (hidden_share - early)),
        down_late.reshape(8 * (hidden_share - early), share),
        preferred_element_type=jnp.float32,
    )
    returned = all_to_all(computed.astype(jnp.bfloat16).reshape(8, CAPACITY, share), CTX)
    block_total = jnp.dot(
        weighing, returned.reshape(8 * CAPACITY, share), preferred_element_type=jnp.float32
    ).astype(jnp.bfloat16)
    parts = all_to_all(block_total.reshape(32, own_tokens, share), EXP)
    expert_total = (
        jnp.sum(parts.reshape(4, 8, own_tokens, share).astype(jnp.float32), axis=0)
        .transpose(1, 0, 2)
        .reshape(own_tokens, width)
    )
    return residual_sum + expert_total


def solution(mesh):
    finer = Mesh(mesh.devices.reshape(SIZES), CTX + EXP)
    return jax.shard_map(
        on_device,
        mesh=finer,
        in_specs=(
            P(CTX, EXP),
            P(CTX, None),
            P(CTX, None),
            P(),
            P(EXP, None, None),
            P(EXP, None, None),
            P(EXP, CTX),
            P(CTX + EXP, None),
            P(),
            P(),
            P(),
            P(None, CTX + EXP),
            P(None, CTX + EXP),
            P(CTX + EXP, None),
        ),
        out_specs=P(CTX + EXP, None),
        check_vma=False,
    )
```

```python
import math

import jax
import jax.numpy as jnp
from jax import lax
from jax.sharding import Mesh, PartitionSpec as P

FF = 2048
CAPACITY = 40
EPSILON = 1e-06

CTX = ("zl", "core")
EXP = ("zh", "x2", "x1", "y")
PATCH = ("x1", "y")
PLANE = ("x2", "x1", "y")
SIZES = (4, 2, 2, 2, 2, 4)


def all_to_all(value, axes):
    return lax.all_to_all(value, axes, split_axis=0, concat_axis=0, tiled=True)


def swap(value, axes, count, mask):
    return lax.ppermute(value, axes, [(i, i ^ mask) for i in range(count)])


def gather_context(value):
    planes = [value] + [swap(value, "zl", 4, mask) for mask in range(1, 4)]
    mine = jnp.stack(planes)
    return jnp.concatenate([mine, swap(mine, "core", 2, 1)])


def sources(here):
    return here ^ jnp.array([0, 2, 4, 6, 1, 3, 5, 7], jnp.int32)


def slots(experts, owners, position):
    matches = experts[:, None, :] == owners[None, :, None]
    chosen = jnp.any(matches, axis=2)
    before = jnp.dot(
        (position[None, :] < position[:, None]).astype(jnp.bfloat16),
        chosen.astype(jnp.bfloat16),
        preferred_element_type=jnp.float32,
    ).astype(jnp.int32)
    columns = jnp.arange(CAPACITY, dtype=jnp.int32)
    return matches, chosen[:, :, None] & (before[:, :, None] == columns)


def attend(queries, latents, rotary_keys, block_order, absorb_key, absorb_value):
    block_size = queries.shape[0]
    head_count, plain_width, latent_width = absorb_key.shape
    rotary_width = rotary_keys.shape[1]
    score_scale = 1.0 / math.sqrt(plain_width + rotary_width)
    keys = gather_context(jnp.concatenate([latents, rotary_keys], axis=1)).reshape(
        8 * block_size, latent_width + rotary_width
    )
    ordered = jnp.arange(block_size, dtype=jnp.int32).reshape(2, 16, 4).transpose(1, 0, 2).reshape(-1)
    shaped = queries.reshape(2, 16, 4, head_count, plain_width + rotary_width)
    shaped = shaped.transpose(1, 0, 2, 3, 4).reshape(
        block_size, head_count, plain_width + rotary_width
    )
    here = lax.axis_index(CTX)
    source_blocks = sources(here)
    source_order = jnp.sum(
        jnp.where(
            jnp.arange(8, dtype=jnp.int32)[None, :] == source_blocks[:, None],
            block_order[None, :],
            0,
        ),
        axis=1,
    )
    row_pos = jnp.tile(source_order[0] * block_size + ordered, head_count)
    key_pos = (
        source_order[:, None] * block_size + jnp.arange(block_size, dtype=jnp.int32)[None, :]
    ).reshape(-1)
    query_latent = jnp.einsum(
        "thn,hnl->htl", shaped[:, :, :plain_width], absorb_key, preferred_element_type=jnp.float32
    ).astype(jnp.bfloat16)
    query = jnp.concatenate(
        [query_latent, shaped[:, :, plain_width:].transpose(1, 0, 2)], axis=2
    ).reshape(head_count * block_size, latent_width + rotary_width)
    scores = (
        jnp.einsum("rl,nl->rn", query, keys, preferred_element_type=jnp.float32) * score_scale
    )
    visible = key_pos[None, :] <= row_pos[:, None]
    scores = jnp.where(visible, scores, -1e30)
    row_max = jnp.max(scores, axis=1, keepdims=True)
    exponent = jnp.where(visible, jnp.exp(scores - row_max), 0.0)
    row_sum = jnp.sum(exponent, axis=1, keepdims=True)
    weighted = jnp.dot(
        exponent.astype(jnp.bfloat16),
        keys[:, :latent_width],
        preferred_element_type=jnp.float32,
    )
    out_latent = (
        (weighted / row_sum).astype(jnp.bfloat16).reshape(head_count, block_size, latent_width)
    )
    return (
        jnp.einsum("htl,hlv->thv", out_latent, absorb_value, preferred_element_type=jnp.float32)
        .astype(jnp.bfloat16)
        .reshape(block_size, -1)
    )


def on_device(
    queries,
    latents,
    rotary_keys,
    block_order,
    absorb_key,
    absorb_value,
    output_weight,
    residual,
    norm_gain,
    route_experts,
    route_weights,
    gate_weight,
    up_weight,
    down_weight,
):
    block_size = queries.shape[0]
    width = norm_gain.shape[0]
    share = output_weight.shape[1]
    hidden_share = gate_weight.shape[1]
    own_tokens = residual.shape[0]
    here = lax.axis_index(CTX)
    member = lax.axis_index(EXP)
    patch_here = lax.axis_index(PATCH)

    early = hidden_share * 5 // 8
    down_early = all_to_all(
        down_weight[:early].reshape(early, 8, share).transpose(1, 0, 2), PATCH
    )

    owners = (here ^ jnp.arange(8, dtype=jnp.int32)) * 4 + member * hidden_share // FF
    own_experts = lax.dynamic_slice_in_dim(route_experts, here * block_size, block_size, 0)
    own_weights = lax.dynamic_slice_in_dim(route_weights, here * block_size, block_size, 0)
    beside = lax.axis_index("x2")
    row = jnp.arange(block_size, dtype=jnp.int32)
    arrival = row % 4 + row // 4 % 2 * 64 + row // 8 % 8 * 4 + (row // 64 ^ beside) * 32
    arrival_experts = own_experts.reshape(2, 2, 8, 4, -1).transpose(1, 2, 0, 3, 4)
    arrival_experts = jnp.where(beside > 0, jnp.flip(arrival_experts, 0), arrival_experts)
    arrival_experts = arrival_experts.reshape(own_experts.shape)
    arranged = slots(arrival_experts, owners, arrival)[1].astype(jnp.bfloat16)
    matches, selected = slots(own_experts, owners, row)
    gate_share = jnp.sum(jnp.where(matches, own_weights[:, None, :], 0.0), axis=2)
    weighing = jnp.where(selected, gate_share[:, :, None], 0.0).astype(jnp.bfloat16)
    weighing = weighing.reshape(block_size, 8 * CAPACITY)

    head_values = attend(queries, latents, rotary_keys, block_order, absorb_key, absorb_value)
    gathered = gather_context(head_values)
    gathered = (
        gathered.reshape(8, 16, 8, -1).transpose(1, 0, 2, 3).reshape(8 * block_size, -1)
    )
    projected = jnp.dot(gathered, output_weight, preferred_element_type=jnp.float32).astype(
        jnp.bfloat16
    )
    projected, down_early, residual_here = lax.optimization_barrier(
        (projected, down_early, residual)
    )
    residual_beside = swap(residual_here, "zh", 2, 1)
    landed = all_to_all(projected.reshape(16, 64, share), PLANE)
    late_rows = down_weight[early:].reshape(hidden_share - early, 8, share).transpose(1, 0, 2)
    landed, late_rows, arranged, weighing, residual_beside = lax.optimization_barrier(
        (landed, late_rows, arranged, weighing, residual_beside)
    )
    partial = jnp.sum(landed.astype(jnp.float32), axis=0).astype(jnp.bfloat16)
    summed = partial.astype(jnp.float32) + swap(partial, "zh", 2, 1).astype(jnp.float32)
    summed = summed.astype(jnp.bfloat16).reshape(8, 2 * own_tokens, share)
    columns_of = jnp.stack([summed[:4], swap(summed[4:], "core", 2, 1)], axis=1)
    columns_of = jnp.stack(
        [columns_of[0]] + [swap(columns_of[mask], "zl", 4, mask) for mask in range(1, 4)]
    ).reshape(2, 2, 2, 2 * own_tokens, share)
    for axis, bit in ((0, 4), (1, 2), (2, 1)):
        columns_of = jnp.where((here & bit) > 0, jnp.flip(columns_of, axis), columns_of)
    rows = columns_of.transpose(3, 0, 1, 2, 4).reshape(2 * own_tokens, width).astype(jnp.float32)
    half = lax.axis_index("zh")
    both_residuals = jnp.concatenate(
        [
            jnp.where(half > 0, residual_beside, residual),
            jnp.where(half > 0, residual, residual_beside),
        ]
    )
    both_sums = rows + both_residuals.astype(jnp.float32)
    residual_sum = lax.dynamic_slice_in_dim(both_sums, half * own_tokens, own_tokens, 0)
    normed = (
        both_sums
        * lax.rsqrt(jnp.mean(both_sums * both_sums, axis=1, keepdims=True) + EPSILON)
        * norm_gain.astype(jnp.float32)
    ).astype(jnp.bfloat16)

    columns = normed.reshape(2 * own_tokens, 8, share).transpose(1, 0, 2)
    group_columns = all_to_all(columns, PATCH).reshape(block_size // 2, share)
    block_columns = jnp.concatenate([group_columns, swap(group_columns, "x2", 2, 1)])

    outgoing = jnp.einsum(
        "trc,td->rcd",
        arranged,
        block_columns,
        preferred_element_type=jnp.float32,
    ).astype(jnp.bfloat16)
    outgoing, late_rows = lax.optimization_barrier((outgoing, late_rows))
    down_late = all_to_all(late_rows, PATCH)
    outgoing = outgoing.reshape(4, 2, CAPACITY, share)
    by_plane = jnp.stack([outgoing[:, 0], swap(outgoing[:, 1], "core", 2, 1)], axis=1)
    by_plane = [by_plane[0]] + [swap(by_plane[mask], "zl", 4, mask) for mask in range(1, 4)]
    arrived = jnp.concatenate(by_plane).reshape(8 * CAPACITY, share)
    arrived, down_late = lax.optimization_barrier((arrived, down_late))

    split = 192
    beside_all = swap(arrived, "x1", 2, 1)
    first_pieces = [arrived[:split]] + [swap(arrived[:split], "y", 4, mask) for mask in range(1, 4)]
    first_pieces = (
        first_pieces
        + [beside_all[:split]]
        + [swap(piece, "x1", 2, 1) for piece in first_pieces[1:]]
    )
    pair = jnp.stack([arrived[split:], beside_all[split:]])
    pairs = [pair] + [swap(pair, "y", 4, mask) for mask in range(1, 4)]
    last_pieces = [both[0] for both in pairs] + [both[1] for both in pairs]

    weights = []
    for mask in range(8):
        first = (patch_here ^ mask) * share
        weights.append(
            jnp.concatenate(
                [
                    lax.dynamic_slice_in_dim(gate_weight, first, share, 0),
                    lax.dynamic_slice_in_dim(up_weight, first, share, 0),
                ],
                axis=1,
            )
        )

    def activate(pieces):
        pre = 0.0
        for piece, weight in zip(pieces, weights):
            pre = pre + jnp.dot(piece, weight, preferred_element_type=jnp.float32)
        return (jax.nn.silu(pre[:, :hidden_share]) * pre[:, hidden_share:]).astype(jnp.bfloat16)

    activated = jnp.concatenate([activate(first_pieces), activate(last_pieces)])
    hidden = all_to_all(
        jnp.broadcast_to(activated[None], (8,) + activated.shape), PATCH
    ).transpose(1, 0, 2)
    computed = jnp.dot(
        hidden[:, :, :early].reshape(8 * CAPACITY, 8 * early),
        down_early.reshape(8 * early, share),
        preferred_element_type=jnp.float32,
    ) + jnp.dot(
        hidden[:, :, early:].reshape(8 * CAPACITY, 8 * (hidden_share - early)),
        down_late.reshape(8 * (hidden_share - early), share),
        preferred_element_type=jnp.float32,
    )
    back = computed.astype(jnp.bfloat16).reshape(4, 2, CAPACITY, share)
    back = jnp.stack([back[0]] + [swap(back[mask], "zl", 4, mask) for mask in range(1, 4)])
    returned = jnp.stack([back[:, 0], swap(back[:, 1], "core", 2, 1)], axis=1)
    block_total = jnp.dot(
        weighing, returned.reshape(8 * CAPACITY, share), preferred_element_type=jnp.float32
    ).astype(jnp.bfloat16)
    parts = all_to_all(block_total.reshape(32, own_tokens, share), EXP)
    expert_total = (
        jnp.sum(parts.reshape(4, 8, own_tokens, share).astype(jnp.float32), axis=0)
        .transpose(1, 0, 2)
        .reshape(own_tokens, width)
    )
    return residual_sum + expert_total


def solution(mesh):
    finer = Mesh(mesh.devices.reshape(SIZES), CTX + EXP)
    return jax.shard_map(
        on_device,
        mesh=finer,
        in_specs=(
            P(CTX, EXP),
            P(CTX, None),
            P(CTX, None),
            P(),
            P(EXP, None, None),
            P(EXP, None, None),
            P(EXP, CTX),
            P(CTX + EXP, None),
            P(),
            P(),
            P(),
            P(None, CTX + EXP),
            P(None, CTX + EXP),
            P(CTX + EXP, None),
        ),
        out_specs=P(CTX + EXP, None),
        check_vma=False,
    )
```

```python
import math

import jax
import jax.numpy as jnp
from jax import lax
from jax.sharding import Mesh, PartitionSpec as P

FF = 2048
CAPACITY = 40
EPSILON = 1e-06

CTX = ("zl", "core")
EXP = ("zh", "x2", "x1", "y")
PATCH = ("x1", "y")
PLANE = ("x2", "x1", "y")
SIZES = (4, 2, 2, 2, 2, 4)


def all_to_all(value, axes):
    return lax.all_to_all(value, axes, split_axis=0, concat_axis=0, tiled=True)


def swap(value, axes, count, mask):
    return lax.ppermute(value, axes, [(i, i ^ mask) for i in range(count)])


def gather_context(value):
    planes = [value] + [swap(value, "zl", 4, mask) for mask in range(1, 4)]
    mine = jnp.stack(planes)
    return jnp.concatenate([mine, swap(mine, "core", 2, 1)])


def sources(here):
    return here ^ jnp.array([0, 2, 4, 6, 1, 3, 5, 7], jnp.int32)


def slots(experts, owners, position):
    matches = experts[:, None, :] == owners[None, :, None]
    chosen = jnp.any(matches, axis=2)
    before = jnp.dot(
        (position[None, :] < position[:, None]).astype(jnp.bfloat16),
        chosen.astype(jnp.bfloat16),
        preferred_element_type=jnp.float32,
    ).astype(jnp.int32)
    columns = jnp.arange(CAPACITY, dtype=jnp.int32)
    return matches, chosen[:, :, None] & (before[:, :, None] == columns)


def attend(queries, latents, rotary_keys, block_order, absorb_key, absorb_value):
    block_size = queries.shape[0]
    head_count, plain_width, latent_width = absorb_key.shape
    rotary_width = rotary_keys.shape[1]
    score_scale = 1.0 / math.sqrt(plain_width + rotary_width)
    keys = gather_context(jnp.concatenate([latents, rotary_keys], axis=1)).reshape(
        8 * block_size, latent_width + rotary_width
    )
    ordered = jnp.arange(block_size, dtype=jnp.int32).reshape(2, 16, 4).transpose(1, 0, 2).reshape(-1)
    shaped = queries.reshape(2, 16, 4, head_count, plain_width + rotary_width)
    shaped = shaped.transpose(1, 0, 2, 3, 4).reshape(
        block_size, head_count, plain_width + rotary_width
    )
    here = lax.axis_index(CTX)
    source_blocks = sources(here)
    source_order = jnp.sum(
        jnp.where(
            jnp.arange(8, dtype=jnp.int32)[None, :] == source_blocks[:, None],
            block_order[None, :],
            0,
        ),
        axis=1,
    )
    row_pos = jnp.tile(source_order[0] * block_size + ordered, head_count)
    key_pos = (
        source_order[:, None] * block_size + jnp.arange(block_size, dtype=jnp.int32)[None, :]
    ).reshape(-1)
    query_latent = jnp.einsum(
        "thn,hnl->htl", shaped[:, :, :plain_width], absorb_key, preferred_element_type=jnp.float32
    ).astype(jnp.bfloat16)
    query = jnp.concatenate(
        [query_latent, shaped[:, :, plain_width:].transpose(1, 0, 2)], axis=2
    ).reshape(head_count * block_size, latent_width + rotary_width)
    scores = (
        jnp.einsum("rl,nl->rn", query, keys, preferred_element_type=jnp.float32) * score_scale
    )
    visible = key_pos[None, :] <= row_pos[:, None]
    scores = jnp.where(visible, scores, -1e30)
    row_max = jnp.max(scores, axis=1, keepdims=True)
    exponent = jnp.where(visible, jnp.exp(scores - row_max), 0.0)
    row_sum = jnp.sum(exponent, axis=1, keepdims=True)
    weighted = jnp.dot(
        exponent.astype(jnp.bfloat16),
        keys[:, :latent_width],
        preferred_element_type=jnp.float32,
    )
    out_latent = (
        (weighted / row_sum).astype(jnp.bfloat16).reshape(head_count, block_size, latent_width)
    )
    return (
        jnp.einsum("htl,hlv->thv", out_latent, absorb_value, preferred_element_type=jnp.float32)
        .astype(jnp.bfloat16)
        .reshape(block_size, -1)
    )


def on_device(
    queries,
    latents,
    rotary_keys,
    block_order,
    absorb_key,
    absorb_value,
    output_weight,
    residual,
    norm_gain,
    route_experts,
    route_weights,
    gate_weight,
    up_weight,
    down_weight,
):
    block_size = queries.shape[0]
    width = norm_gain.shape[0]
    share = output_weight.shape[1]
    hidden_share = gate_weight.shape[1]
    own_tokens = residual.shape[0]
    here = lax.axis_index(CTX)
    member = lax.axis_index(EXP)
    patch_here = lax.axis_index(PATCH)

    early = hidden_share * 9 // 16
    down_early = all_to_all(
        down_weight[:early].reshape(early, 8, share).transpose(1, 0, 2), PATCH
    )

    owners = (here ^ jnp.arange(8, dtype=jnp.int32)) * 4 + member * hidden_share // FF
    own_experts = lax.dynamic_slice_in_dim(route_experts, here * block_size, block_size, 0)
    own_weights = lax.dynamic_slice_in_dim(route_weights, here * block_size, block_size, 0)
    beside = lax.axis_index("x2")
    row = jnp.arange(block_size, dtype=jnp.int32)
    arrival = row % 4 + row // 4 % 2 * 64 + row // 8 % 8 * 4 + (row // 64 ^ beside) * 32
    arrival_experts = own_experts.reshape(2, 2, 8, 4, -1).transpose(1, 2, 0, 3, 4)
    arrival_experts = jnp.where(beside > 0, jnp.flip(arrival_experts, 0), arrival_experts)
    arrival_experts = arrival_experts.reshape(own_experts.shape)
    arranged = slots(arrival_experts, owners, arrival)[1].astype(jnp.bfloat16)
    matches, selected = slots(own_experts, owners, row)
    gate_share = jnp.sum(jnp.where(matches, own_weights[:, None, :], 0.0), axis=2)
    weighing = jnp.where(selected, gate_share[:, :, None], 0.0).astype(jnp.bfloat16)
    weighing = weighing.reshape(block_size, 8 * CAPACITY)

    head_values = attend(queries, latents, rotary_keys, block_order, absorb_key, absorb_value)
    gathered = gather_context(head_values)
    gathered = (
        gathered.reshape(8, 16, 8, -1).transpose(1, 0, 2, 3).reshape(8 * block_size, -1)
    )
    projected = jnp.dot(gathered, output_weight, preferred_element_type=jnp.float32).astype(
        jnp.bfloat16
    )
    projected, down_early, residual_here = lax.optimization_barrier(
        (projected, down_early, residual)
    )
    residual_beside = swap(residual_here, "zh", 2, 1)
    landed = all_to_all(projected.reshape(16, 64, share), PLANE)
    late_rows = down_weight[early:].reshape(hidden_share - early, 8, share).transpose(1, 0, 2)
    landed, late_rows, arranged, weighing, residual_beside = lax.optimization_barrier(
        (landed, late_rows, arranged, weighing, residual_beside)
    )
    partial = jnp.sum(landed.astype(jnp.float32), axis=0).astype(jnp.bfloat16)
    partial = partial.reshape(2, 4, 2 * own_tokens, share)
    pieces = jnp.stack([partial[0], swap(partial[1], "core", 2, 1)], axis=1)
    pieces = pieces.reshape(2, 2, 2, 2 * own_tokens, share)
    for axis, bit in ((0, 4), (1, 2)):
        pieces = jnp.where((here & bit) > 0, jnp.flip(pieces, axis), pieces)
    pieces = jnp.broadcast_to(
        pieces.reshape(4, 1, 2, 2 * own_tokens, share), (4, 2, 2, 2 * own_tokens, share)
    ).reshape(8, 2, 2 * own_tokens, share)
    pieces = all_to_all(pieces, ("zl", "zh")).reshape(4, 2, 2, 2 * own_tokens, share)
    summed = pieces[:, 0].astype(jnp.float32) + pieces[:, 1].astype(jnp.float32)
    summed = jnp.where((here & 1) > 0, jnp.flip(summed, 1), summed)
    rows = summed.transpose(2, 0, 1, 3).reshape(2 * own_tokens, width)
    half = lax.axis_index("zh")
    both_residuals = jnp.concatenate(
        [
            jnp.where(half > 0, residual_beside, residual),
            jnp.where(half > 0, residual, residual_beside),
        ]
    )
    both_sums = rows + both_residuals.astype(jnp.float32)
    residual_sum = lax.dynamic_slice_in_dim(both_sums, half * own_tokens, own_tokens, 0)
    normed = (
        both_sums
        * lax.rsqrt(jnp.mean(both_sums * both_sums, axis=1, keepdims=True) + EPSILON)
        * norm_gain.astype(jnp.float32)
    ).astype(jnp.bfloat16)

    columns = normed.reshape(2 * own_tokens, 8, share).transpose(1, 0, 2)
    group_columns = all_to_all(columns, PATCH).reshape(block_size // 2, share)
    block_columns = jnp.concatenate([group_columns, swap(group_columns, "x2", 2, 1)])

    outgoing = jnp.einsum(
        "trc,td->rcd",
        arranged,
        block_columns,
        preferred_element_type=jnp.float32,
    ).astype(jnp.bfloat16)
    outgoing, late_rows = lax.optimization_barrier((outgoing, late_rows))
    down_late = all_to_all(late_rows, PATCH)
    outgoing = outgoing.reshape(4, 2, CAPACITY, share)
    by_plane = jnp.stack([outgoing[:, 0], swap(outgoing[:, 1], "core", 2, 1)], axis=1)
    by_plane = [by_plane[0]] + [swap(by_plane[mask], "zl", 4, mask) for mask in range(1, 4)]
    arrived = jnp.concatenate(by_plane).reshape(8 * CAPACITY, share)
    arrived, down_late = lax.optimization_barrier((arrived, down_late))
    down_columns = jnp.concatenate([down_early, down_late], axis=1).reshape(-1, share)

    split = 192
    beside_all = swap(arrived, "x1", 2, 1)
    first_pieces = [arrived[:split]] + [swap(arrived[:split], "y", 4, mask) for mask in range(1, 4)]
    first_pieces = (
        first_pieces
        + [beside_all[:split]]
        + [swap(piece, "x1", 2, 1) for piece in first_pieces[1:]]
    )
    pair = jnp.stack([arrived[split:], beside_all[split:]])
    pairs = [pair] + [swap(pair, "y", 4, mask) for mask in range(1, 4)]
    last_pieces = [both[0] for both in pairs] + [both[1] for both in pairs]

    weights = []
    for mask in range(8):
        first = (patch_here ^ mask) * share
        weights.append(
            jnp.concatenate(
                [
                    lax.dynamic_slice_in_dim(gate_weight, first, share, 0),
                    lax.dynamic_slice_in_dim(up_weight, first, share, 0),
                ],
                axis=1,
            )
        )

    def activate(pieces):
        pre = 0.0
        for piece, weight in zip(pieces, weights):
            pre = pre + jnp.dot(piece, weight, preferred_element_type=jnp.float32)
        return (jax.nn.silu(pre[:, :hidden_share]) * pre[:, hidden_share:]).astype(jnp.bfloat16)

    activated = jnp.concatenate([activate(first_pieces), activate(last_pieces)])
    hidden = all_to_all(
        jnp.broadcast_to(activated[None], (8,) + activated.shape), PATCH
    ).transpose(1, 0, 2)
    computed = jnp.dot(
        hidden.reshape(8 * CAPACITY, 8 * hidden_share),
        down_columns,
        preferred_element_type=jnp.float32,
    )
    back = computed.astype(jnp.bfloat16).reshape(4, 2, CAPACITY, share)
    back = jnp.stack([back[0]] + [swap(back[mask], "zl", 4, mask) for mask in range(1, 4)])
    returned = jnp.stack([back[:, 0], swap(back[:, 1], "core", 2, 1)], axis=1)
    block_total = jnp.dot(
        weighing, returned.reshape(8 * CAPACITY, share), preferred_element_type=jnp.float32
    ).astype(jnp.bfloat16)
    parts = all_to_all(block_total.reshape(32, own_tokens, share), EXP)
    expert_total = (
        jnp.sum(parts.reshape(4, 8, own_tokens, share).astype(jnp.float32), axis=0)
        .transpose(1, 0, 2)
        .reshape(own_tokens, width)
    )
    return residual_sum + expert_total


def solution(mesh):
    finer = Mesh(mesh.devices.reshape(SIZES), CTX + EXP)
    return jax.shard_map(
        on_device,
        mesh=finer,
        in_specs=(
            P(CTX, EXP),
            P(CTX, None),
            P(CTX, None),
            P(),
            P(EXP, None, None),
            P(EXP, None, None),
            P(EXP, CTX),
            P(CTX + EXP, None),
            P(),
            P(),
            P(),
            P(None, CTX + EXP),
            P(None, CTX + EXP),
            P(CTX + EXP, None),
        ),
        out_specs=P(CTX + EXP, None),
        check_vma=False,
    )
```

```python
import math

import jax
import jax.numpy as jnp
from jax import lax
from jax.sharding import Mesh, PartitionSpec as P

FF = 2048
CAPACITY = 40
EPSILON = 1e-06

CTX = ("zl", "core")
EXP = ("zh", "x2", "x1", "y")
PATCH = ("x1", "y")
PLANE = ("x2", "x1", "y")
SIZES = (4, 2, 2, 2, 2, 4)


def all_to_all(value, axes):
    return lax.all_to_all(value, axes, split_axis=0, concat_axis=0, tiled=True)


def swap(value, axes, count, mask):
    return lax.ppermute(value, axes, [(i, i ^ mask) for i in range(count)])


def gather_context(value):
    planes = [value] + [swap(value, "zl", 4, mask) for mask in range(1, 4)]
    mine = jnp.stack(planes)
    return jnp.concatenate([mine, swap(mine, "core", 2, 1)])


def sources(here):
    return here ^ jnp.array([0, 2, 4, 6, 1, 3, 5, 7], jnp.int32)


def slots(experts, owners, position):
    matches = experts[:, None, :] == owners[None, :, None]
    chosen = jnp.any(matches, axis=2)
    before = jnp.dot(
        (position[None, :] < position[:, None]).astype(jnp.bfloat16),
        chosen.astype(jnp.bfloat16),
        preferred_element_type=jnp.float32,
    ).astype(jnp.int32)
    columns = jnp.arange(CAPACITY, dtype=jnp.int32)
    return matches, chosen[:, :, None] & (before[:, :, None] == columns)


def attend(queries, latents, rotary_keys, block_order, absorb_key, absorb_value):
    block_size = queries.shape[0]
    head_count, plain_width, latent_width = absorb_key.shape
    rotary_width = rotary_keys.shape[1]
    score_scale = 1.0 / math.sqrt(plain_width + rotary_width)
    keys = gather_context(jnp.concatenate([latents, rotary_keys], axis=1)).reshape(
        8 * block_size, latent_width + rotary_width
    )
    ordered = jnp.arange(block_size, dtype=jnp.int32).reshape(2, 16, 4).transpose(1, 0, 2).reshape(-1)
    shaped = queries.reshape(2, 16, 4, head_count, plain_width + rotary_width)
    shaped = shaped.transpose(1, 0, 2, 3, 4).reshape(
        block_size, head_count, plain_width + rotary_width
    )
    here = lax.axis_index(CTX)
    source_blocks = sources(here)
    source_order = jnp.sum(
        jnp.where(
            jnp.arange(8, dtype=jnp.int32)[None, :] == source_blocks[:, None],
            block_order[None, :],
            0,
        ),
        axis=1,
    )
    row_pos = jnp.tile(source_order[0] * block_size + ordered, head_count)
    key_pos = (
        source_order[:, None] * block_size + jnp.arange(block_size, dtype=jnp.int32)[None, :]
    ).reshape(-1)
    query_latent = jnp.einsum(
        "thn,hnl->htl", shaped[:, :, :plain_width], absorb_key, preferred_element_type=jnp.float32
    ).astype(jnp.bfloat16)
    query = jnp.concatenate(
        [query_latent, shaped[:, :, plain_width:].transpose(1, 0, 2)], axis=2
    ).reshape(head_count * block_size, latent_width + rotary_width)
    scores = (
        jnp.einsum("rl,nl->rn", query, keys, preferred_element_type=jnp.float32) * score_scale
    )
    visible = key_pos[None, :] <= row_pos[:, None]
    scores = jnp.where(visible, scores, -1e30)
    row_max = jnp.max(scores, axis=1, keepdims=True)
    exponent = jnp.where(visible, jnp.exp(scores - row_max), 0.0)
    row_sum = jnp.sum(exponent, axis=1, keepdims=True)
    weighted = jnp.dot(
        exponent.astype(jnp.bfloat16),
        keys[:, :latent_width],
        preferred_element_type=jnp.float32,
    )
    out_latent = (
        (weighted / row_sum).astype(jnp.bfloat16).reshape(head_count, block_size, latent_width)
    )
    return (
        jnp.einsum("htl,hlv->thv", out_latent, absorb_value, preferred_element_type=jnp.float32)
        .astype(jnp.bfloat16)
        .reshape(block_size, -1)
    )


def on_device(
    queries,
    latents,
    rotary_keys,
    block_order,
    absorb_key,
    absorb_value,
    output_weight,
    residual,
    norm_gain,
    route_experts,
    route_weights,
    gate_weight,
    up_weight,
    down_weight,
):
    block_size = queries.shape[0]
    width = norm_gain.shape[0]
    share = output_weight.shape[1]
    hidden_share = gate_weight.shape[1]
    own_tokens = residual.shape[0]
    here = lax.axis_index(CTX)
    member = lax.axis_index(EXP)
    patch_here = lax.axis_index(PATCH)

    early = hidden_share * 9 // 16
    down_early = all_to_all(
        down_weight[:early].reshape(early, 8, share).transpose(1, 0, 2), PATCH
    )

    owners = (here ^ jnp.arange(8, dtype=jnp.int32)) * 4 + member * hidden_share // FF
    own_experts = lax.dynamic_slice_in_dim(route_experts, here * block_size, block_size, 0)
    own_weights = lax.dynamic_slice_in_dim(route_weights, here * block_size, block_size, 0)
    row = jnp.arange(block_size, dtype=jnp.int32)
    arrival = row % 4 + row // 4 % 2 * 64 + row // 8 % 8 * 4 + row // 64 * 32
    arrival_experts = own_experts.reshape(2, 2, 8, 4, -1).transpose(1, 2, 0, 3, 4)
    arrival_experts = arrival_experts.reshape(own_experts.shape)
    arranged = slots(arrival_experts, owners, arrival)[1].astype(jnp.bfloat16)
    matches, selected = slots(own_experts, owners, row)
    gate_share = jnp.sum(jnp.where(matches, own_weights[:, None, :], 0.0), axis=2)
    weighing = jnp.where(selected, gate_share[:, :, None], 0.0).astype(jnp.bfloat16)
    weighing = weighing.reshape(block_size, 8 * CAPACITY)

    head_values = attend(queries, latents, rotary_keys, block_order, absorb_key, absorb_value)
    gathered = gather_context(head_values)
    gathered = (
        gathered.reshape(8, 16, 8, -1).transpose(1, 0, 2, 3).reshape(8 * block_size, -1)
    )
    projected = jnp.dot(gathered, output_weight, preferred_element_type=jnp.float32).astype(
        jnp.bfloat16
    )
    projected, down_early, residual_here = lax.optimization_barrier(
        (projected, down_early, residual)
    )
    residual_beside = swap(residual_here, "zh", 2, 1)
    landed = all_to_all(projected.reshape(16, 64, share), PLANE)
    late_rows = down_weight[early:].reshape(hidden_share - early, 8, share).transpose(1, 0, 2)
    landed, late_rows, arranged, weighing, residual_beside = lax.optimization_barrier(
        (landed, late_rows, arranged, weighing, residual_beside)
    )
    partial = jnp.sum(landed.astype(jnp.float32), axis=0).astype(jnp.bfloat16)
    partial = partial.reshape(2, 4, 2 * own_tokens, share)
    pieces = jnp.stack([partial[0], swap(partial[1], "core", 2, 1)], axis=1)
    pieces = pieces.reshape(2, 2, 2, 2 * own_tokens, share)
    for axis, bit in ((0, 4), (1, 2)):
        pieces = jnp.where((here & bit) > 0, jnp.flip(pieces, axis), pieces)
    pieces = jnp.broadcast_to(
        pieces.reshape(4, 1, 2, 2 * own_tokens, share), (4, 2, 2, 2 * own_tokens, share)
    ).reshape(8, 2, 2 * own_tokens, share)
    pieces = all_to_all(pieces, ("zl", "zh")).reshape(4, 2, 2, 2 * own_tokens, share)
    summed = pieces[:, 0].astype(jnp.float32) + pieces[:, 1].astype(jnp.float32)
    summed = jnp.where((here & 1) > 0, jnp.flip(summed, 1), summed)
    rows = summed.transpose(2, 0, 1, 3).reshape(2 * own_tokens, width)
    half = lax.axis_index("zh")
    both_residuals = jnp.concatenate(
        [
            jnp.where(half > 0, residual_beside, residual),
            jnp.where(half > 0, residual, residual_beside),
        ]
    )
    both_sums = rows + both_residuals.astype(jnp.float32)
    residual_sum = lax.dynamic_slice_in_dim(both_sums, half * own_tokens, own_tokens, 0)
    normed = (
        both_sums
        * lax.rsqrt(jnp.mean(both_sums * both_sums, axis=1, keepdims=True) + EPSILON)
        * norm_gain.astype(jnp.float32)
    ).astype(jnp.bfloat16)

    columns = normed.reshape(2 * own_tokens, 8, share).transpose(1, 0, 2)
    spread = jnp.broadcast_to(columns[None], (2,) + columns.shape)
    block_columns = all_to_all(
        spread.reshape(16, 2 * own_tokens, share), PLANE
    ).reshape(block_size, share)

    outgoing = jnp.einsum(
        "trc,td->rcd",
        arranged,
        block_columns,
        preferred_element_type=jnp.float32,
    ).astype(jnp.bfloat16)
    outgoing, late_rows = lax.optimization_barrier((outgoing, late_rows))
    down_late = all_to_all(late_rows, PATCH)
    outgoing = outgoing.reshape(4, 2, CAPACITY, share)
    by_plane = jnp.stack([outgoing[:, 0], swap(outgoing[:, 1], "core", 2, 1)], axis=1)
    by_plane = [by_plane[0]] + [swap(by_plane[mask], "zl", 4, mask) for mask in range(1, 4)]
    arrived = jnp.concatenate(by_plane).reshape(8 * CAPACITY, share)
    arrived, down_late = lax.optimization_barrier((arrived, down_late))
    down_columns = jnp.concatenate([down_early, down_late], axis=1).reshape(-1, share)

    split = 192
    beside_all = swap(arrived, "x1", 2, 1)
    first_pieces = [arrived[:split]] + [swap(arrived[:split], "y", 4, mask) for mask in range(1, 4)]
    first_pieces = (
        first_pieces
        + [beside_all[:split]]
        + [swap(piece, "x1", 2, 1) for piece in first_pieces[1:]]
    )
    pair = jnp.stack([arrived[split:], beside_all[split:]])
    pairs = [pair] + [swap(pair, "y", 4, mask) for mask in range(1, 4)]
    last_pieces = [both[0] for both in pairs] + [both[1] for both in pairs]

    weights = []
    for mask in range(8):
        first = (patch_here ^ mask) * share
        weights.append(
            jnp.concatenate(
                [
                    lax.dynamic_slice_in_dim(gate_weight, first, share, 0),
                    lax.dynamic_slice_in_dim(up_weight, first, share, 0),
                ],
                axis=1,
            )
        )

    def activate(pieces):
        pre = 0.0
        for piece, weight in zip(pieces, weights):
            pre = pre + jnp.dot(piece, weight, preferred_element_type=jnp.float32)
        return (jax.nn.silu(pre[:, :hidden_share]) * pre[:, hidden_share:]).astype(jnp.bfloat16)

    activated = jnp.concatenate([activate(first_pieces), activate(last_pieces)])
    hidden = all_to_all(
        jnp.broadcast_to(activated[None], (8,) + activated.shape), PATCH
    ).transpose(1, 0, 2)
    computed = jnp.dot(
        hidden.reshape(8 * CAPACITY, 8 * hidden_share),
        down_columns,
        preferred_element_type=jnp.float32,
    )
    back = computed.astype(jnp.bfloat16).reshape(4, 2, CAPACITY, share)
    back = jnp.stack([back[0]] + [swap(back[mask], "zl", 4, mask) for mask in range(1, 4)])
    returned = jnp.stack([back[:, 0], swap(back[:, 1], "core", 2, 1)], axis=1)
    block_total = jnp.dot(
        weighing, returned.reshape(8 * CAPACITY, share), preferred_element_type=jnp.float32
    ).astype(jnp.bfloat16)
    parts = all_to_all(block_total.reshape(32, own_tokens, share), EXP)
    expert_total = (
        jnp.sum(parts.reshape(4, 8, own_tokens, share).astype(jnp.float32), axis=0)
        .transpose(1, 0, 2)
        .reshape(own_tokens, width)
    )
    return residual_sum + expert_total


def solution(mesh):
    finer = Mesh(mesh.devices.reshape(SIZES), CTX + EXP)
    return jax.shard_map(
        on_device,
        mesh=finer,
        in_specs=(
            P(CTX, EXP),
            P(CTX, None),
            P(CTX, None),
            P(),
            P(EXP, None, None),
            P(EXP, None, None),
            P(EXP, CTX),
            P(CTX + EXP, None),
            P(),
            P(),
            P(),
            P(None, CTX + EXP),
            P(None, CTX + EXP),
            P(CTX + EXP, None),
        ),
        out_specs=P(CTX + EXP, None),
        check_vma=False,
    )
```

```python
import math

import jax
import jax.numpy as jnp
from jax import lax
from jax.sharding import Mesh, PartitionSpec as P

FF = 2048
CAPACITY = 40
EPSILON = 1e-06

CTX = ("zl", "core")
EXP = ("zh", "x2", "x1", "y")
PATCH = ("x1", "y")
PLANE = ("x2", "x1", "y")
SIZES = (4, 2, 2, 2, 2, 4)


def all_to_all(value, axes):
    return lax.all_to_all(value, axes, split_axis=0, concat_axis=0, tiled=True)


def swap(value, axes, count, mask):
    return lax.ppermute(value, axes, [(i, i ^ mask) for i in range(count)])


def gather_context(value):
    planes = [value] + [swap(value, "zl", 4, mask) for mask in range(1, 4)]
    mine = jnp.stack(planes)
    return jnp.concatenate([mine, swap(mine, "core", 2, 1)])


def sources(here):
    return here ^ jnp.array([0, 2, 4, 6, 1, 3, 5, 7], jnp.int32)


def slots(experts, owners, position):
    matches = experts[:, None, :] == owners[None, :, None]
    chosen = jnp.any(matches, axis=2)
    before = jnp.dot(
        (position[None, :] < position[:, None]).astype(jnp.bfloat16),
        chosen.astype(jnp.bfloat16),
        preferred_element_type=jnp.float32,
    ).astype(jnp.int32)
    columns = jnp.arange(CAPACITY, dtype=jnp.int32)
    return matches, chosen[:, :, None] & (before[:, :, None] == columns)


def attend(queries, latents, rotary_keys, block_order, absorb_key, absorb_value):
    block_size = queries.shape[0]
    head_count, plain_width, latent_width = absorb_key.shape
    rotary_width = rotary_keys.shape[1]
    score_scale = 1.0 / math.sqrt(plain_width + rotary_width)
    keys = gather_context(jnp.concatenate([latents, rotary_keys], axis=1)).reshape(
        8 * block_size, latent_width + rotary_width
    )
    ordered = jnp.arange(block_size, dtype=jnp.int32).reshape(2, 16, 4).transpose(1, 0, 2).reshape(-1)
    shaped = queries.reshape(2, 16, 4, head_count, plain_width + rotary_width)
    shaped = shaped.transpose(1, 0, 2, 3, 4).reshape(
        block_size, head_count, plain_width + rotary_width
    )
    here = lax.axis_index(CTX)
    source_blocks = sources(here)
    source_order = jnp.sum(
        jnp.where(
            jnp.arange(8, dtype=jnp.int32)[None, :] == source_blocks[:, None],
            block_order[None, :],
            0,
        ),
        axis=1,
    )
    row_pos = jnp.tile(source_order[0] * block_size + ordered, head_count)
    key_pos = (
        source_order[:, None] * block_size + jnp.arange(block_size, dtype=jnp.int32)[None, :]
    ).reshape(-1)
    query_latent = jnp.einsum(
        "thn,hnl->htl", shaped[:, :, :plain_width], absorb_key, preferred_element_type=jnp.float32
    ).astype(jnp.bfloat16)
    query = jnp.concatenate(
        [query_latent, shaped[:, :, plain_width:].transpose(1, 0, 2)], axis=2
    ).reshape(head_count * block_size, latent_width + rotary_width)
    scores = (
        jnp.einsum("rl,nl->rn", query, keys, preferred_element_type=jnp.float32) * score_scale
    )
    visible = key_pos[None, :] <= row_pos[:, None]
    scores = jnp.where(visible, scores, -1e30)
    row_max = jnp.max(scores, axis=1, keepdims=True)
    exponent = jnp.where(visible, jnp.exp(scores - row_max), 0.0)
    row_sum = jnp.sum(exponent, axis=1, keepdims=True)
    weighted = jnp.dot(
        exponent.astype(jnp.bfloat16),
        keys[:, :latent_width],
        preferred_element_type=jnp.float32,
    )
    out_latent = (
        (weighted / row_sum).astype(jnp.bfloat16).reshape(head_count, block_size, latent_width)
    )
    return (
        jnp.einsum("htl,hlv->thv", out_latent, absorb_value, preferred_element_type=jnp.float32)
        .astype(jnp.bfloat16)
        .reshape(block_size, -1)
    )


def on_device(
    queries,
    latents,
    rotary_keys,
    block_order,
    absorb_key,
    absorb_value,
    output_weight,
    residual,
    norm_gain,
    route_experts,
    route_weights,
    gate_weight,
    up_weight,
    down_weight,
):
    block_size = queries.shape[0]
    width = norm_gain.shape[0]
    share = output_weight.shape[1]
    hidden_share = gate_weight.shape[1]
    own_tokens = residual.shape[0]
    here = lax.axis_index(CTX)
    member = lax.axis_index(EXP)
    patch_here = lax.axis_index(PATCH)

    early = hidden_share // 2
    down_early = all_to_all(
        down_weight[:early].reshape(early, 8, share).transpose(1, 0, 2), PATCH
    )

    owners = (here ^ jnp.arange(8, dtype=jnp.int32)) * 4 + member * hidden_share // FF
    own_experts = lax.dynamic_slice_in_dim(route_experts, here * block_size, block_size, 0)
    own_weights = lax.dynamic_slice_in_dim(route_weights, here * block_size, block_size, 0)
    row = jnp.arange(block_size, dtype=jnp.int32)
    arrival = row % 4 + row // 4 % 2 * 64 + row // 8 % 8 * 4 + row // 64 * 32
    arrival_experts = own_experts.reshape(2, 2, 8, 4, -1).transpose(1, 2, 0, 3, 4)
    arrival_experts = arrival_experts.reshape(own_experts.shape)
    arranged = slots(arrival_experts, owners, arrival)[1].astype(jnp.bfloat16)
    matches, selected = slots(own_experts, owners, row)
    gate_share = jnp.sum(jnp.where(matches, own_weights[:, None, :], 0.0), axis=2)
    weighing = jnp.where(selected, gate_share[:, :, None], 0.0).astype(jnp.bfloat16)
    weighing = weighing.reshape(block_size, 8 * CAPACITY)

    head_values = attend(queries, latents, rotary_keys, block_order, absorb_key, absorb_value)
    gathered = gather_context(head_values)
    gathered = (
        gathered.reshape(8, 16, 8, -1).transpose(1, 0, 2, 3).reshape(8 * block_size, -1)
    )
    projected = jnp.dot(gathered, output_weight, preferred_element_type=jnp.float32).astype(
        jnp.bfloat16
    )
    projected, down_early, residual_here = lax.optimization_barrier(
        (projected, down_early, residual)
    )
    residual_beside = swap(residual_here, "zh", 2, 1)
    landed = all_to_all(projected.reshape(16, 64, share), PLANE)
    late_rows = down_weight[early:].reshape(hidden_share - early, 8, share).transpose(1, 0, 2)
    landed, late_rows, arranged, weighing, residual_beside = lax.optimization_barrier(
        (landed, late_rows, arranged, weighing, residual_beside)
    )
    partial = jnp.sum(landed.astype(jnp.float32), axis=0).astype(jnp.bfloat16)
    partial = partial.reshape(2, 4, 2 * own_tokens, share)
    pieces = jnp.stack([partial[0], swap(partial[1], "core", 2, 1)], axis=1)
    pieces = pieces.reshape(2, 2, 2, 2 * own_tokens, share)
    for axis, bit in ((0, 4), (1, 2)):
        pieces = jnp.where((here & bit) > 0, jnp.flip(pieces, axis), pieces)
    pieces = jnp.broadcast_to(
        pieces.reshape(4, 1, 2, 2 * own_tokens, share), (4, 2, 2, 2 * own_tokens, share)
    ).reshape(8, 2, 2 * own_tokens, share)
    pieces = all_to_all(pieces, ("zl", "zh")).reshape(4, 2, 2, 2 * own_tokens, share)
    summed = pieces[:, 0].astype(jnp.float32) + pieces[:, 1].astype(jnp.float32)
    summed = jnp.where((here & 1) > 0, jnp.flip(summed, 1), summed)
    rows = summed.transpose(2, 0, 1, 3).reshape(2 * own_tokens, width)
    half = lax.axis_index("zh")
    both_residuals = jnp.concatenate(
        [
            jnp.where(half > 0, residual_beside, residual),
            jnp.where(half > 0, residual, residual_beside),
        ]
    )
    both_sums = rows + both_residuals.astype(jnp.float32)
    residual_sum = lax.dynamic_slice_in_dim(both_sums, half * own_tokens, own_tokens, 0)
    normed = (
        both_sums
        * lax.rsqrt(jnp.mean(both_sums * both_sums, axis=1, keepdims=True) + EPSILON)
        * norm_gain.astype(jnp.float32)
    ).astype(jnp.bfloat16)

    columns = normed.reshape(2 * own_tokens, 8, share).transpose(1, 0, 2)
    spread = jnp.broadcast_to(columns[None], (2,) + columns.shape)
    block_columns = all_to_all(
        spread.reshape(16, 2 * own_tokens, share), PLANE
    ).reshape(block_size, share)

    outgoing = jnp.einsum(
        "trc,td->rcd",
        arranged,
        block_columns,
        preferred_element_type=jnp.float32,
    ).astype(jnp.bfloat16)
    outgoing, late_rows = lax.optimization_barrier((outgoing, late_rows))
    down_late = all_to_all(late_rows, PATCH)
    outgoing = outgoing.reshape(4, 2, CAPACITY, share)
    by_plane = jnp.stack([outgoing[:, 0], swap(outgoing[:, 1], "core", 2, 1)], axis=1)
    by_plane = [by_plane[0]] + [swap(by_plane[mask], "zl", 4, mask) for mask in range(1, 4)]
    arrived = jnp.concatenate(by_plane).reshape(8 * CAPACITY, share)
    arrived, down_late = lax.optimization_barrier((arrived, down_late))
    down_columns = jnp.concatenate([down_early, down_late], axis=1).reshape(-1, share)

    split = 192
    beside_all = swap(arrived, "x1", 2, 1)
    first_pieces = [arrived[:split]] + [swap(arrived[:split], "y", 4, mask) for mask in range(1, 4)]
    first_pieces = (
        first_pieces
        + [beside_all[:split]]
        + [swap(piece, "x1", 2, 1) for piece in first_pieces[1:]]
    )
    pair = jnp.stack([arrived[split:], beside_all[split:]])
    pairs = [pair] + [swap(pair, "y", 4, mask) for mask in range(1, 4)]
    last_pieces = [both[0] for both in pairs] + [both[1] for both in pairs]

    weights = []
    for mask in range(8):
        first = (patch_here ^ mask) * share
        weights.append(
            jnp.concatenate(
                [
                    lax.dynamic_slice_in_dim(gate_weight, first, share, 0),
                    lax.dynamic_slice_in_dim(up_weight, first, share, 0),
                ],
                axis=1,
            )
        )

    def activate(pieces):
        pre = 0.0
        for piece, weight in zip(pieces, weights):
            pre = pre + jnp.dot(piece, weight, preferred_element_type=jnp.float32)
        return (jax.nn.silu(pre[:, :hidden_share]) * pre[:, hidden_share:]).astype(jnp.bfloat16)

    activated = jnp.concatenate([activate(first_pieces), activate(last_pieces)])
    hidden = all_to_all(
        jnp.broadcast_to(activated[None], (8,) + activated.shape), PATCH
    ).transpose(1, 0, 2)
    computed = jnp.dot(
        hidden.reshape(8 * CAPACITY, 8 * hidden_share),
        down_columns,
        preferred_element_type=jnp.float32,
    )
    back = computed.astype(jnp.bfloat16).reshape(4, 2, CAPACITY, share)
    back = jnp.stack([back[0]] + [swap(back[mask], "zl", 4, mask) for mask in range(1, 4)])
    returned = jnp.stack([back[:, 0], swap(back[:, 1], "core", 2, 1)], axis=1)
    block_total = jnp.dot(
        weighing, returned.reshape(8 * CAPACITY, share), preferred_element_type=jnp.float32
    ).astype(jnp.bfloat16)
    parts = all_to_all(block_total.reshape(32, own_tokens, share), EXP)
    expert_total = (
        jnp.sum(parts.reshape(4, 8, own_tokens, share).astype(jnp.float32), axis=0)
        .transpose(1, 0, 2)
        .reshape(own_tokens, width)
    )
    return residual_sum + expert_total


def solution(mesh):
    finer = Mesh(mesh.devices.reshape(SIZES), CTX + EXP)
    return jax.shard_map(
        on_device,
        mesh=finer,
        in_specs=(
            P(CTX, EXP),
            P(CTX, None),
            P(CTX, None),
            P(),
            P(EXP, None, None),
            P(EXP, None, None),
            P(EXP, CTX),
            P(CTX + EXP, None),
            P(),
            P(),
            P(),
            P(None, CTX + EXP),
            P(None, CTX + EXP),
            P(CTX + EXP, None),
        ),
        out_specs=P(CTX + EXP, None),
        check_vma=False,
    )
```

```python
import math

import jax
import jax.numpy as jnp
from jax import lax
from jax.sharding import Mesh, PartitionSpec as P

FF = 2048
CAPACITY = 40
EPSILON = 1e-06

CTX = ("zl", "core")
EXP = ("zh", "x2", "x1", "y")
PATCH = ("x1", "y")
PLANE = ("x2", "x1", "y")
SIZES = (4, 2, 2, 2, 2, 4)


def all_to_all(value, axes):
    return lax.all_to_all(value, axes, split_axis=0, concat_axis=0, tiled=True)


def swap(value, axes, count, mask):
    return lax.ppermute(value, axes, [(i, i ^ mask) for i in range(count)])


def gather_context(value):
    planes = [value] + [swap(value, "zl", 4, mask) for mask in range(1, 4)]
    mine = jnp.stack(planes)
    return jnp.concatenate([mine, swap(mine, "core", 2, 1)])


def sources(here):
    return here ^ jnp.array([0, 2, 4, 6, 1, 3, 5, 7], jnp.int32)


def slots(experts, owners, position):
    matches = experts[:, None, :] == owners[None, :, None]
    chosen = jnp.any(matches, axis=2)
    before = jnp.dot(
        (position[None, :] < position[:, None]).astype(jnp.bfloat16),
        chosen.astype(jnp.bfloat16),
        preferred_element_type=jnp.float32,
    ).astype(jnp.int32)
    columns = jnp.arange(CAPACITY, dtype=jnp.int32)
    return matches, chosen[:, :, None] & (before[:, :, None] == columns)


def attend(queries, latents, rotary_keys, block_order, absorb_key, absorb_value):
    block_size = queries.shape[0]
    head_count, plain_width, latent_width = absorb_key.shape
    rotary_width = rotary_keys.shape[1]
    score_scale = 1.0 / math.sqrt(plain_width + rotary_width)
    keys = gather_context(jnp.concatenate([latents, rotary_keys], axis=1)).reshape(
        8 * block_size, latent_width + rotary_width
    )
    ordered = jnp.arange(block_size, dtype=jnp.int32).reshape(2, 16, 4).transpose(1, 0, 2).reshape(-1)
    shaped = queries.reshape(2, 16, 4, head_count, plain_width + rotary_width)
    shaped = shaped.transpose(1, 0, 2, 3, 4).reshape(
        block_size, head_count, plain_width + rotary_width
    )
    here = lax.axis_index(CTX)
    source_blocks = sources(here)
    source_order = jnp.sum(
        jnp.where(
            jnp.arange(8, dtype=jnp.int32)[None, :] == source_blocks[:, None],
            block_order[None, :],
            0,
        ),
        axis=1,
    )
    row_pos = jnp.tile(source_order[0] * block_size + ordered, head_count)
    key_pos = (
        source_order[:, None] * block_size + jnp.arange(block_size, dtype=jnp.int32)[None, :]
    ).reshape(-1)
    query_latent = jnp.einsum(
        "thn,hnl->htl", shaped[:, :, :plain_width], absorb_key, preferred_element_type=jnp.float32
    ).astype(jnp.bfloat16)
    query = jnp.concatenate(
        [query_latent, shaped[:, :, plain_width:].transpose(1, 0, 2)], axis=2
    ).reshape(head_count * block_size, latent_width + rotary_width)
    scores = (
        jnp.einsum("rl,nl->rn", query, keys, preferred_element_type=jnp.float32) * score_scale
    )
    visible = key_pos[None, :] <= row_pos[:, None]
    scores = jnp.where(visible, scores, -1e30)
    row_max = jnp.max(scores, axis=1, keepdims=True)
    exponent = jnp.where(visible, jnp.exp(scores - row_max), 0.0)
    row_sum = jnp.sum(exponent, axis=1, keepdims=True)
    weighted = jnp.dot(
        exponent.astype(jnp.bfloat16),
        keys[:, :latent_width],
        preferred_element_type=jnp.float32,
    )
    out_latent = (
        (weighted / row_sum).astype(jnp.bfloat16).reshape(head_count, block_size, latent_width)
    )
    return (
        jnp.einsum("htl,hlv->thv", out_latent, absorb_value, preferred_element_type=jnp.float32)
        .astype(jnp.bfloat16)
        .reshape(block_size, -1)
    )


def on_device(
    queries,
    latents,
    rotary_keys,
    block_order,
    absorb_key,
    absorb_value,
    output_weight,
    residual,
    norm_gain,
    route_experts,
    route_weights,
    gate_weight,
    up_weight,
    down_weight,
):
    block_size = queries.shape[0]
    width = norm_gain.shape[0]
    share = output_weight.shape[1]
    hidden_share = gate_weight.shape[1]
    own_tokens = residual.shape[0]
    here = lax.axis_index(CTX)
    member = lax.axis_index(EXP)
    patch_here = lax.axis_index(PATCH)

    early = hidden_share * 9 // 16
    down_early = all_to_all(
        down_weight[:early].reshape(early, 8, share).transpose(1, 0, 2), PATCH
    )

    owners = (here ^ jnp.arange(8, dtype=jnp.int32)) * 4 + member * hidden_share // FF
    own_experts = lax.dynamic_slice_in_dim(route_experts, here * block_size, block_size, 0)
    own_weights = lax.dynamic_slice_in_dim(route_weights, here * block_size, block_size, 0)
    row = jnp.arange(block_size, dtype=jnp.int32)
    arrival = row % 4 + row // 4 % 2 * 64 + row // 8 % 8 * 4 + row // 64 * 32
    arrival_experts = own_experts.reshape(2, 2, 8, 4, -1).transpose(1, 2, 0, 3, 4)
    arrival_experts = arrival_experts.reshape(own_experts.shape)
    arranged = slots(arrival_experts, owners, arrival)[1].astype(jnp.bfloat16)
    matches, selected = slots(own_experts, owners, row)
    gate_share = jnp.sum(jnp.where(matches, own_weights[:, None, :], 0.0), axis=2)
    weighing = jnp.where(selected, gate_share[:, :, None], 0.0).astype(jnp.bfloat16)
    weighing = weighing.reshape(block_size, 8 * CAPACITY)

    head_values = attend(queries, latents, rotary_keys, block_order, absorb_key, absorb_value)
    gathered = gather_context(head_values)
    gathered = (
        gathered.reshape(8, 16, 8, -1).transpose(1, 0, 2, 3).reshape(8 * block_size, -1)
    )
    projected = jnp.dot(gathered, output_weight, preferred_element_type=jnp.float32).astype(
        jnp.bfloat16
    )
    projected, down_early, residual_here = lax.optimization_barrier(
        (projected, down_early, residual)
    )
    residual_beside = swap(residual_here, "zh", 2, 1)
    landed = all_to_all(projected.reshape(16, 64, share), PLANE)
    late_rows = down_weight[early:].reshape(hidden_share - early, 8, share).transpose(1, 0, 2)
    landed, late_rows, arranged, weighing, residual_beside = lax.optimization_barrier(
        (landed, late_rows, arranged, weighing, residual_beside)
    )
    partial = jnp.sum(landed.astype(jnp.float32), axis=0).astype(jnp.bfloat16)
    partial = partial.reshape(2, 4, 2 * own_tokens, share)
    pieces = jnp.stack([partial[0], swap(partial[1], "core", 2, 1)], axis=1)
    pieces = pieces.reshape(2, 2, 2, 2 * own_tokens, share)
    for axis, bit in ((0, 4), (1, 2)):
        pieces = jnp.where((here & bit) > 0, jnp.flip(pieces, axis), pieces)
    pieces = jnp.broadcast_to(
        pieces.reshape(4, 1, 2, 2 * own_tokens, share), (4, 2, 2, 2 * own_tokens, share)
    ).reshape(8, 2, 2 * own_tokens, share)
    pieces = all_to_all(pieces, ("zl", "zh")).reshape(4, 2, 2, 2 * own_tokens, share)
    summed = pieces[:, 0].astype(jnp.float32) + pieces[:, 1].astype(jnp.float32)
    summed = jnp.where((here & 1) > 0, jnp.flip(summed, 1), summed)
    rows = summed.transpose(2, 0, 1, 3).reshape(2 * own_tokens, width)
    half = lax.axis_index("zh")
    both_residuals = jnp.concatenate(
        [
            jnp.where(half > 0, residual_beside, residual),
            jnp.where(half > 0, residual, residual_beside),
        ]
    )
    both_sums = rows + both_residuals.astype(jnp.float32)
    residual_sum = lax.dynamic_slice_in_dim(both_sums, half * own_tokens, own_tokens, 0)
    normed = (
        both_sums
        * lax.rsqrt(jnp.mean(both_sums * both_sums, axis=1, keepdims=True) + EPSILON)
        * norm_gain.astype(jnp.float32)
    ).astype(jnp.bfloat16)

    columns = normed.reshape(2 * own_tokens, 8, share).transpose(1, 0, 2)
    spread = jnp.broadcast_to(columns[None], (2,) + columns.shape)
    block_columns = all_to_all(
        spread.reshape(16, 2 * own_tokens, share), PLANE
    ).reshape(block_size, share)

    outgoing = jnp.einsum(
        "trc,td->rcd",
        arranged,
        block_columns,
        preferred_element_type=jnp.float32,
    ).astype(jnp.bfloat16)
    outgoing, late_rows = lax.optimization_barrier((outgoing, late_rows))
    down_late = all_to_all(late_rows, PATCH)
    outgoing = outgoing.reshape(4, 2, CAPACITY, share)
    by_plane = jnp.stack([outgoing[:, 0], swap(outgoing[:, 1], "core", 2, 1)], axis=1)
    by_plane = [by_plane[0]] + [swap(by_plane[mask], "zl", 4, mask) for mask in range(1, 4)]
    arrived = jnp.concatenate(by_plane).reshape(8 * CAPACITY, share)
    arrived, down_late = lax.optimization_barrier((arrived, down_late))
    down_columns = jnp.concatenate([down_early, down_late], axis=1).reshape(-1, share)

    split = 192
    first, last = arrived[:split], arrived[split:]
    pair = jnp.stack([last, swap(last, "x1", 2, 1)])
    first_pieces = [first] + [swap(first, "y", 4, mask) for mask in range(1, 4)]
    first_pieces = first_pieces + [swap(piece, "x1", 2, 1) for piece in first_pieces]
    pairs = [pair] + [swap(pair, "y", 4, mask) for mask in range(1, 4)]
    last_pieces = [both[0] for both in pairs] + [both[1] for both in pairs]

    weights = []
    for mask in range(8):
        first = (patch_here ^ mask) * share
        weights.append(
            jnp.concatenate(
                [
                    lax.dynamic_slice_in_dim(gate_weight, first, share, 0),
                    lax.dynamic_slice_in_dim(up_weight, first, share, 0),
                ],
                axis=1,
            )
        )

    def activate(pieces):
        pre = 0.0
        for piece, weight in zip(pieces, weights):
            pre = pre + jnp.dot(piece, weight, preferred_element_type=jnp.float32)
        return (jax.nn.silu(pre[:, :hidden_share]) * pre[:, hidden_share:]).astype(jnp.bfloat16)

    activated = jnp.concatenate([activate(first_pieces), activate(last_pieces)])
    hidden = all_to_all(
        jnp.broadcast_to(activated[None], (8,) + activated.shape), PATCH
    ).transpose(1, 0, 2)
    computed = jnp.dot(
        hidden.reshape(8 * CAPACITY, 8 * hidden_share),
        down_columns,
        preferred_element_type=jnp.float32,
    )
    back = computed.astype(jnp.bfloat16).reshape(4, 2, CAPACITY, share)
    back = jnp.stack([back[0]] + [swap(back[mask], "zl", 4, mask) for mask in range(1, 4)])
    returned = jnp.stack([back[:, 0], swap(back[:, 1], "core", 2, 1)], axis=1)
    block_total = jnp.dot(
        weighing, returned.reshape(8 * CAPACITY, share), preferred_element_type=jnp.float32
    ).astype(jnp.bfloat16)
    parts = all_to_all(block_total.reshape(32, own_tokens, share), EXP)
    expert_total = (
        jnp.sum(parts.reshape(4, 8, own_tokens, share).astype(jnp.float32), axis=0)
        .transpose(1, 0, 2)
        .reshape(own_tokens, width)
    )
    return residual_sum + expert_total


def solution(mesh):
    finer = Mesh(mesh.devices.reshape(SIZES), CTX + EXP)
    return jax.shard_map(
        on_device,
        mesh=finer,
        in_specs=(
            P(CTX, EXP),
            P(CTX, None),
            P(CTX, None),
            P(),
            P(EXP, None, None),
            P(EXP, None, None),
            P(EXP, CTX),
            P(CTX + EXP, None),
            P(),
            P(),
            P(),
            P(None, CTX + EXP),
            P(None, CTX + EXP),
            P(CTX + EXP, None),
        ),
        out_specs=P(CTX + EXP, None),
        check_vma=False,
    )
```
